32 devices in a mesh: img: 4 (over y, x), seq: 8 (over z, core).
Axes of the slice: x: 2, y: 2, z: 4, core: 2. Of those that a mesh axis runs over, the one named last changes fastest.
Arguments:
- query_proj: bfloat16 [4, 1024, 1280], P('img', 'seq'), may hold values from -6 to 6
- key_proj: bfloat16 [4, 1024, 1280], P('img', 'seq'), may hold values from -6 to 6
- value_proj: bfloat16 [4, 1024, 1280], P('img', 'seq'), may hold values from -12 to 12
- merge_cells: int32 [4, 256, 4], P('img', 'seq'), may hold values from 0 to 1023, as said below
- unmerge: int32 [4, 1024], P('img', 'seq'), may hold values from 0 to 255, as said below
- grad_out: bfloat16 [4, 1024, 1280], P('img', 'seq'), may hold values from -9 to 9
- query_gain: float32 [64], replicated, may hold values from 1 to 2.5
- key_gain: float32 [64], replicated, may hold values from 1 to 2.5
Outputs:
- attended: bfloat16 [4, 1024, 1280], P('img', 'seq')
- grad_query: bfloat16 [4, 1024, 1280], P('img', 'seq')
- grad_key: bfloat16 [4, 1024, 1280], P('img', 'seq')
- grad_value: bfloat16 [4, 1024, 1280], P('img', 'seq')
- grad_query_gain: float32 [64], replicated
- grad_key_gain: float32 [64], replicated
The draws below stay inside these ranges and needn't reach their ends.
Inputs may be any that keep to these rules, and one draw needn't show every extreme that they name: `merge_cells`: row c of an image lists, in some order, the four tokens of one 2x2 cell: columns j and j + 1 (modulo 64) of image rows 2 i and 2 i + 1, where token r * 64 + s stands at row r and column s and j has one parity within each pair of rows; every token lies in exactly one cell; cell c and its four tokens are held by the same seq index. `unmerge`: entry t is the row of merge_cells of the same image that lists token t.
All inputs are finite; a program needn't handle non-finite values.
Results may differ from the reference program's by a relative error of at most 0.012.
Values may be sent and summed in bfloat16 or wider, within the bound.
No kernel may reach another device: no remote copies, remote signals or barrier semaphores. Data moves between devices by JAX's collectives and lax.ppermute only.
A program may use at most 128 MiB of HBM per device.

```python
import math
import jax
import jax.numpy as jnp
from jax import lax

HD = 64
H = 20
COLS = 64
HE = 1280
TOK_DEV = 128
TOKENS = 1024
C_DEV = 32
CELLS = 256
IMAGES = 4


def cell_layout(key):
    pair_count = TOKENS // (2 * COLS)
    half_cols = COLS // 2
    devices = TOKENS // TOK_DEV
    col_phase = jax.random.randint(jax.random.fold_in(key, 3), (pair_count, 1), 0, 2)
    pair_ids = jnp.arange(pair_count, dtype=jnp.int32)[:, None]
    col_slot = jnp.arange(half_cols, dtype=jnp.int32)[None, :]
    left_col = (2 * col_slot + col_phase) % COLS
    right_col = (2 * col_slot + 1 + col_phase) % COLS
    top_token = 2 * pair_ids * COLS
    cell_tokens = jnp.stack([top_token + left_col, top_token + right_col, top_token + COLS + left_col, top_token + COLS + right_col], axis=-1).reshape(CELLS, 4)
    rotation = jax.random.randint(jax.random.fold_in(key, 4), (CELLS, 1), 0, 4)
    entry_order = (jnp.arange(4, dtype=jnp.int32)[None, :] + rotation) % 4
    cell_tokens = jnp.take_along_axis(cell_tokens, entry_order, axis=1)
    sub_keys = jax.random.split(jax.random.fold_in(key, 5), devices)
    permuted = jax.vmap(lambda sub_key: jax.random.permutation(sub_key, C_DEV))(sub_keys)
    cell_slots = (permuted.astype(jnp.int32) + (jnp.arange(devices, dtype=jnp.int32) * C_DEV)[:, None]).reshape(CELLS)
    merge_table = jnp.zeros((CELLS, 4), jnp.int32).at[cell_slots].set(cell_tokens)
    unmerge_table = jnp.zeros((TOKENS,), jnp.int32).at[cell_tokens.reshape(-1)].set(jnp.repeat(cell_slots, 4))
    return (merge_table, unmerge_table)


def draw_merge_cells(key, part):
    base = jax.random.fold_in(key, 7)
    return jax.vmap(lambda image_index: cell_layout(jax.random.fold_in(base, image_index))[0])(jnp.arange(IMAGES, dtype=jnp.int32))


def draw_unmerge(key, part):
    base = jax.random.fold_in(key, 7)
    return jax.vmap(lambda image_index: cell_layout(jax.random.fold_in(base, image_index))[1])(jnp.arange(IMAGES, dtype=jnp.int32))


def draw_grad_out(key, part):
    noise_vals = jax.random.normal(jax.random.fold_in(key, 11), (IMAGES, TOKENS, HE), jnp.float32)
    position = (jnp.arange(IMAGES, dtype=jnp.float32)[:, None] * TOKENS + jnp.arange(TOKENS, dtype=jnp.float32)[None, :]) / (IMAGES * TOKENS - 1)
    row_scale = 0.5 + position
    return (jnp.clip(noise_vals, -4.0, 4.0) * row_scale[:, :, None]).astype(jnp.bfloat16)


def levels(rng, dims, shards, low, largest):
    def one(axis_at, blocks):
        heights = jax.random.uniform(jax.random.fold_in(jax.random.fold_in(rng, 6), axis_at), (blocks,), jnp.float32, low / len(shards), largest / len(shards))
        return jnp.repeat(jnp.exp(heights), dims[axis_at] // blocks).reshape((-1,) + (1,) * (len(dims) - axis_at - 1))

    gain = one(*shards[0])
    for cut in shards[1:]:
        gain = gain * one(*cut)
    return gain


def bell_draw(stream_key, dims, scale, bound, cuts=(), kind=jnp.bfloat16):
    values = scale * jax.random.normal(stream_key, dims, jnp.float32)
    if cuts:
        values = values * levels(stream_key, dims, cuts, -0.22, 0.18)
    return jnp.clip(values, -bound, bound).astype(kind)


def setup_inputs(seed: int = 0) -> dict:
    streams_of = jax.random.split(jax.random.key(seed), 9)
    return {
        "query_proj": bell_draw(streams_of[0], (IMAGES, TOKENS, HE), 1.0, 6.0, ((0, 4), (1, 8))),
        "key_proj": bell_draw(streams_of[1], (IMAGES, TOKENS, HE), 1.0, 6.0, ((0, 4), (1, 8))),
        "value_proj": bell_draw(streams_of[2], (IMAGES, TOKENS, HE), 2.0, 12.0, ((0, 4), (1, 8))),
        "merge_cells": draw_merge_cells(jax.random.fold_in(streams_of[8], 71), 0),
        "unmerge": draw_unmerge(jax.random.fold_in(streams_of[8], 71), 0),
        "grad_out": draw_grad_out(jax.random.fold_in(streams_of[8], 71), 0),
        "query_gain": jnp.clip(jnp.exp(jax.random.uniform(streams_of[6], (HD,), jnp.float32, math.log(1.0), math.log(2.5))), 1.0, 2.5),
        "key_gain": jnp.clip(jnp.exp(jax.random.uniform(streams_of[7], (HD,), jnp.float32, math.log(1.0), math.log(2.5))), 1.0, 2.5),
    }


EPSILON = 1e-06

def normalize(inputs, gain_row):
    row_scale = lax.rsqrt(lax.optimization_barrier(jnp.mean(inputs * inputs, axis=-1, keepdims=True)) + EPSILON)
    unit_vals = inputs * row_scale
    return (unit_vals, row_scale, unit_vals * gain_row)

def norm_back(grad_normed, unit_vals, row_scale, gain_row):
    grad_unit = grad_normed * gain_row
    mean_inner = lax.optimization_barrier(jnp.mean(grad_unit * unit_vals, axis=-1, keepdims=True))
    return row_scale * (grad_unit - unit_vals * mean_inner)

def head_pass(pieces):
    queries, key_rows, value_rows, upstream = pieces
    scores = jnp.dot(queries, key_rows.T, preferred_element_type=jnp.float32) * 0.125
    exp_scores = jnp.exp(scores)
    row_total = lax.optimization_barrier(jnp.sum(exp_scores, axis=1, keepdims=True))
    attended = (jnp.dot(exp_scores.astype(jnp.bfloat16), value_rows, preferred_element_type=jnp.float32) / row_total).astype(jnp.bfloat16)
    attention = exp_scores / row_total
    grad_values = jnp.dot(attention.astype(jnp.bfloat16).T, upstream, preferred_element_type=jnp.float32)
    grad_weights = jnp.dot(upstream, value_rows.T, preferred_element_type=jnp.float32)
    row_inner = lax.optimization_barrier(jnp.sum(upstream.astype(jnp.float32) * attended.astype(jnp.float32), axis=1, keepdims=True))
    grad_scores = (attention * (grad_weights - row_inner)).astype(jnp.bfloat16)
    grad_queries = jnp.dot(grad_scores, key_rows, preferred_element_type=jnp.float32) * 0.125
    grad_keys = jnp.dot(grad_scores.T, queries, preferred_element_type=jnp.float32) * 0.125
    return (attended, grad_queries, grad_keys, grad_values)

def by_head(array, row_count):
    return array.reshape(row_count, H, HD).transpose(1, 0, 2)

def one_image(pieces, query_gain, key_gain):
    query_proj, key_proj, value_proj, merge_cells, unmerge, grad_out = pieces
    q_unit, q_scale, q_normed = normalize(query_proj.astype(jnp.float32).reshape(TOKENS, H, HD), query_gain)
    q_bf = q_normed.astype(jnp.bfloat16)
    k_unit, k_scale, k_normed = normalize(key_proj.astype(jnp.float32).reshape(TOKENS, H, HD), key_gain)
    k_flat = k_normed.reshape(TOKENS, HE)
    k_merged = (lax.optimization_barrier(jnp.sum(k_flat[merge_cells], axis=1)) * 0.25).astype(jnp.bfloat16)
    v_merged = (lax.optimization_barrier(jnp.sum(value_proj.astype(jnp.float32)[merge_cells], axis=1)) * 0.25).astype(jnp.bfloat16)
    results = lax.map(head_pass, (q_bf.transpose(1, 0, 2), by_head(k_merged, CELLS), by_head(v_merged, CELLS), by_head(grad_out, TOKENS)))
    attended = results[0].transpose(1, 0, 2).reshape(TOKENS, HE)
    grad_q_normed = results[1].transpose(1, 0, 2)
    grad_merged_k = results[2].transpose(1, 0, 2).reshape(CELLS, HE)
    grad_merged_v = results[3].transpose(1, 0, 2).reshape(CELLS, HE)
    grad_k_normed = (0.25 * grad_merged_k[unmerge]).reshape(TOKENS, H, HD)
    grad_value = (0.25 * grad_merged_v[unmerge]).astype(jnp.bfloat16)
    query_part = lax.optimization_barrier(jnp.sum(grad_q_normed * q_unit, axis=(0, 1)))
    key_part = lax.optimization_barrier(jnp.sum(grad_k_normed * k_unit, axis=(0, 1)))
    grad_query = norm_back(grad_q_normed, q_unit, q_scale, query_gain).reshape(TOKENS, HE).astype(jnp.bfloat16)
    grad_key = norm_back(grad_k_normed, k_unit, k_scale, key_gain).reshape(TOKENS, HE).astype(jnp.bfloat16)
    return (attended, grad_query, grad_key, grad_value, query_part, key_part)

def reference(query_proj, key_proj, value_proj, merge_cells, unmerge, grad_out, query_gain, key_gain):

    def image_pass(pieces):
        return one_image(pieces, query_gain, key_gain)
    results = lax.map(image_pass, (query_proj, key_proj, value_proj, merge_cells, unmerge, grad_out))
    return (results[0], results[1], results[2], results[3], lax.optimization_barrier(jnp.sum(results[4], axis=0)), lax.optimization_barrier(jnp.sum(results[5], axis=0)))
```

```python
import functools
import math

import jax
import jax.numpy as jnp
from jax import lax
from jax.experimental import pallas as pl
from jax.experimental.pallas import tpu as pltpu
from jax.sharding import PartitionSpec as P

EPSILON = 1e-06
TILE = 128
CORES = 2
BF16 = jnp.bfloat16
F32 = jnp.float32
VMEM_BYTES = 40 * 1024 * 1024


def call(kernel, out_shapes, inputs, scratch=()):
    in_vmem = pl.BlockSpec(memory_space=pltpu.VMEM)
    return pl.pallas_call(
        kernel,
        out_shape=[jax.ShapeDtypeStruct(shape, kind) for shape, kind in out_shapes],
        in_specs=[in_vmem] * len(inputs),
        out_specs=[in_vmem] * len(out_shapes),
        scratch_shapes=[pltpu.VMEM(shape, kind) for shape, kind in scratch],
        compiler_params=pltpu.CompilerParams(vmem_limit_bytes=VMEM_BYTES),
    )(*inputs)


def core_side():
    return lax.rem(lax.axis_index("seq"), CORES)


def lanes_at(index):
    return pl.ds(pl.multiple_of(index * TILE, TILE), TILE)


def dot(left, right, contract=((1,), (0,))):
    return lax.dot_general(left, right, (contract, ((), ())), preferred_element_type=F32)


def halves(array):
    high = array.astype(BF16)
    return high, (array - high.astype(F32)).astype(BF16)


def exact_dot(left, right, contract=((1,), (0,))):
    high, low = halves(right)
    return dot(left, high, contract) + dot(left, low, contract)


def head_mean(array, head_dim):
    rows = lax.broadcasted_iota(jnp.int32, (TILE, TILE), 0) // head_dim
    cols = lax.broadcasted_iota(jnp.int32, (TILE, TILE), 1) // head_dim
    same = jnp.where(rows == cols, 1.0 / head_dim, 0.0).astype(BF16)
    high, low = halves(array)
    return dot(high, same) + dot(low, same)


def unit_rows(array, head_dim):
    scale = lax.rsqrt(head_mean(array * array, head_dim) + EPSILON)
    return array * scale, scale


def norm_back(grad_normed, unit_vals, scale, gain_row, head_dim):
    grad_unit = grad_normed * gain_row
    return scale * (grad_unit - unit_vals * head_mean(grad_unit * unit_vals, head_dim))


def merge_kernel(head_dim, bounds, key_ref, value_ref, cells_ref, gain_ref, *refs):
    count = len(bounds)
    own_refs, send_refs, merged = refs[:count], refs[count : 2 * count], refs[2 * count :]
    tok, lanes = key_ref.shape
    half = lanes // CORES
    cells = cells_ref.shape[0]
    side = core_side()
    listed = lax.rem(cells_ref[...], tok)
    ids = lax.broadcasted_iota(jnp.int32, (cells, tok), 1)
    member = sum(
        (listed[:, j : j + 1] == ids).astype(F32) for j in range(cells_ref.shape[1])
    ).astype(BF16)
    gain_row = gain_ref[...] * 0.25
    for part in range(CORES):
        for chunk, (start, stop) in enumerate(bounds):
            for at in range(start, stop, TILE):
                source = slice(part * half + at, part * half + at + TILE)
                unit_vals, _ = unit_rows(key_ref[:, source].astype(F32), head_dim)
                keys = exact_dot(member, unit_vals) * gain_row
                values = dot(member, value_ref[:, source]) * 0.25
                merged[chunk][part, :, at - start : at - start + TILE] = keys.astype(BF16)
                there = stop - start + at - start
                merged[chunk][part, :, there : there + TILE] = values.astype(BF16)
    for chunk in range(count):
        own_refs[chunk][...] = merged[chunk][side]
        send_refs[chunk][...] = merged[chunk][1 - side]


def pack_kernel(query_ref, upstream_ref, send_ref):
    half = query_ref.shape[1] // CORES
    other = 1 - core_side()
    for tile in range(half // TILE):
        source = lanes_at(other * (half // TILE) + tile)
        send_ref[:, tile * TILE : (tile + 1) * TILE] = query_ref[:, source]
        send_ref[:, half + tile * TILE : half + (tile + 1) * TILE] = upstream_ref[:, source]


def query_kernel(head_dim, query_ref, upstream_ref, arrived_ref, gain_ref, out_ref, grad_ref):
    tok, lanes = query_ref.shape
    half = lanes // CORES
    side = core_side()
    for tile in range(half // TILE):
        lane = slice(tile * TILE, (tile + 1) * TILE)
        other = slice(half + tile * TILE, half + (tile + 1) * TILE)
        source = lanes_at(side * (half // TILE) + tile)
        for row, queries in ((0, query_ref[:, source]), (tok, arrived_ref[:, lane])):
            unit_vals, _ = unit_rows(queries.astype(F32), head_dim)
            out_ref[row : row + tok, lane] = (unit_vals * gain_ref[...]).astype(BF16)
        grad_ref[:tok, lane] = upstream_ref[:, source]
        grad_ref[tok:, lane] = arrived_ref[:, other]


def attend_kernel(head_dim, start, blocks, group, *refs):
    query_ref, upstream_ref, gain_ref = refs[:3]
    block_refs = refs[3 : 3 + blocks]
    attended_ref, grad_ref, gain_out_ref = refs[3 + blocks : 6 + blocks]
    part_refs = refs[6 + blocks :]
    rows = query_ref.shape[0]
    block_rows, width = block_refs[0].shape
    width = width // 2
    per = TILE // head_dim
    cells = group * block_rows
    scale = head_dim**-0.5
    exponent = scale * math.log2(math.e)
    lane_head = lax.broadcasted_iota(jnp.int32, (1, TILE), 1) // head_dim
    cell_heads = lax.broadcasted_iota(jnp.int32, (cells, TILE), 1) // head_dim
    masks = [(cell_heads == head).astype(F32).astype(BF16) for head in range(per)]

    def spread(array):
        return jnp.concatenate([array * mask for mask in masks], axis=0)

    def by_lane(parts):
        result = parts[0]
        for head in range(1, per):
            result = jnp.where(lane_head == head, parts[head], result)
        return result

    def folded(array):
        return by_lane([array[head * cells : (head + 1) * cells] for head in range(per)])

    def one_tile(tile, gain_sum):
        lane = lanes_at(tile)
        value_lane = lanes_at(width // TILE + tile)
        source = lanes_at(start // TILE + tile)
        queries = query_ref[:, source]
        upstream = upstream_ref[:, source]
        weighted = jnp.zeros((rows, TILE), F32)
        totals = [jnp.zeros((rows, 1), F32) for _ in range(per)]
        held = []
        for first in range(0, blocks, group):
            members = block_refs[first : first + group]
            keys = jnp.concatenate([ref[:, lane] for ref in members], axis=0)
            spread_keys = spread(keys)
            spread_values = spread(
                jnp.concatenate([ref[:, value_lane] for ref in members], axis=0)
            )
            scores = dot(queries, spread_keys, ((1,), (1,)))
            exp_scores = jnp.exp2(scores * exponent)
            weighted += dot(exp_scores.astype(BF16), spread_values)
            exp_parts = [exp_scores[:, h * cells : (h + 1) * cells] for h in range(per)]
            totals = [
                total + jnp.sum(part, axis=1, keepdims=True)
                for total, part in zip(totals, exp_parts)
            ]
            held.append((keys, spread_keys, spread_values, exp_parts))
        inverses = [1.0 / total for total in totals]
        attended = (weighted * by_lane(inverses)).astype(BF16)
        attended_ref[:, lane] = attended
        products = upstream.astype(F32) * attended.astype(F32)
        inners = [
            jnp.sum(jnp.where(lane_head == h, products, 0.0), axis=1, keepdims=True)
            for h in range(per)
        ]
        grad_queries = jnp.zeros((rows, TILE), F32)
        for index, (keys, spread_keys, spread_values, exp_parts) in enumerate(held):
            grad_weights = dot(upstream, spread_values, ((1,), (1,)))
            attention = [part * inverse for part, inverse in zip(exp_parts, inverses)]
            grad_scores = jnp.concatenate(
                [
                    (attention[h] * (grad_weights[:, h * cells : (h + 1) * cells] - inners[h]))
                    .astype(BF16)
                    for h in range(per)
                ],
                axis=1,
            )
            attention_bf = jnp.concatenate([part.astype(BF16) for part in attention], axis=1)
            grad_queries += dot(grad_scores, spread_keys)
            grad_keys = folded(dot(grad_scores, queries, ((0,), (0,)))) * scale
            grad_values = folded(dot(attention_bf, upstream, ((0,), (0,))))
            gain_sum += jnp.sum(grad_keys * keys.astype(F32), axis=0, keepdims=True)
            for member in range(group):
                ref = part_refs[index * group + member]
                here = slice(member * block_rows, (member + 1) * block_rows)
                ref[:, lane] = grad_keys[here].astype(ref.dtype)
                ref[:, value_lane] = grad_values[here].astype(ref.dtype)
        grad_ref[:, lane] = grad_queries * scale
        return gain_sum

    gain_sum = jnp.zeros((1, TILE), F32)
    if blocks == group:
        for tile in range(width // TILE):
            gain_sum = one_tile(tile, gain_sum)
    else:
        gain_sum = lax.fori_loop(0, width // TILE, one_tile, gain_sum)
    gain_out_ref[...] = gain_sum / gain_ref[...]


def query_back_kernel(head_dim, bounds, query_ref, arrived_ref, gain_ref, *refs):
    count = len(bounds)
    attended_refs, grad_refs, gain_refs = (
        refs[i * count : (i + 1) * count] for i in range(3)
    )
    own_ref, send_ref, gain_out_ref = refs[3 * count :]
    tok, lanes = query_ref.shape
    half = lanes // CORES
    side = core_side()
    query_sum = jnp.zeros((1, TILE), F32)
    for (start, stop), attended_ref, grad_ref in zip(bounds, attended_refs, grad_refs):
        for at in range(start, stop, TILE):
            here = slice(at - start, at - start + TILE)
            lane = slice(at, at + TILE)
            grad_lane = slice(half + at, half + at + TILE)
            source = lanes_at(side * (half // TILE) + at // TILE)
            for row, queries, out_ref in (
                (0, query_ref[:, source], own_ref),
                (tok, arrived_ref[:, lane], send_ref),
            ):
                unit_vals, scale = unit_rows(queries.astype(F32), head_dim)
                grad_normed = grad_ref[row : row + tok, here]
                query_sum += jnp.sum(grad_normed * unit_vals, axis=0, keepdims=True)
                out_ref[:, lane] = attended_ref[row : row + tok, here]
                out_ref[:, grad_lane] = norm_back(
                    grad_normed, unit_vals, scale, gain_ref[...], head_dim
                ).astype(BF16)
    key_sum = gain_refs[0][...]
    for ref in gain_refs[1:]:
        key_sum += ref[...]

    def per_channel(row):
        return sum(row[:, at : at + head_dim] for at in range(0, TILE, head_dim))

    gain_out_ref[...] = jnp.concatenate([per_channel(query_sum), per_channel(key_sum)], axis=1)


def place_kernel(own_ref, arrived_ref, attended_ref, grad_ref):
    half = own_ref.shape[1] // 2
    tiles = half // TILE
    side = core_side()
    for source_ref, at_side in ((own_ref, side), (arrived_ref, 1 - side)):
        for tile in range(tiles):
            there = lanes_at(at_side * tiles + tile)
            attended_ref[:, there] = source_ref[:, tile * TILE : (tile + 1) * TILE]
            grad_ref[:, there] = source_ref[:, half + tile * TILE : half + (tile + 1) * TILE]


def key_back_kernel(head_dim, bounds, terms, key_ref, unmerge_ref, gain_ref, *refs):
    count = len(bounds)
    term_refs = [refs[chunk * terms : (chunk + 1) * terms] for chunk in range(count)]
    arrived_refs = refs[count * terms : count * (terms + 1)]
    grad_key_ref, grad_value_ref = refs[count * (terms + 1) : count * (terms + 1) + 2]
    merged = refs[count * (terms + 1) + 2 :]
    tok, lanes = key_ref.shape
    half = lanes // CORES
    cells = arrived_refs[0].shape[0]
    side = core_side()
    for chunk in range(count):
        total = term_refs[chunk][0][:cells].astype(F32)
        for ref in term_refs[chunk][1:]:
            total += ref[:cells].astype(F32)
        merged[chunk][side] = total
        merged[chunk][1 - side] = arrived_refs[chunk][...]
    owner = lax.rem(unmerge_ref[...], cells)
    table = (lax.broadcasted_iota(jnp.int32, (cells, tok), 0) == owner).astype(F32).astype(BF16)
    for part in range(CORES):
        for chunk, (start, stop) in enumerate(bounds):
            for at in range(start, stop, TILE):
                here = at - start
                there = stop - start + here
                lane = slice(part * half + at, part * half + at + TILE)
                grad_keys = merged[chunk][part, :, here : here + TILE]
                grad_values = merged[chunk][part, :, there : there + TILE]
                unit_vals, scale = unit_rows(key_ref[:, lane].astype(F32), head_dim)
                grad_normed = exact_dot(table, grad_keys, ((0,), (0,))) * 0.25
                grad_key_ref[:, lane] = norm_back(
                    grad_normed, unit_vals, scale, gain_ref[...], head_dim
                ).astype(BF16)
                grad_value_ref[:, lane] = (
                    exact_dot(table, grad_values, ((0,), (0,))) * 0.25
                ).astype(BF16)


def exchange(array, axis, apart):
    return lax.ppermute(array, axis, [(i, i ^ apart) for i in range(lax.axis_size(axis))])


def chip_gather(block, chips):
    if chips == 1:
        return [block]
    mirrored = exchange(block, "seq", CORES * (chips - 1))
    low = chip_gather(block, chips // 2)
    high = chip_gather(mirrored, chips // 2)
    return low + high[::-1]


def chip_reduce(parts):
    chips = len(parts)
    if chips == 1:
        return [parts[0]]
    high = chip_reduce(parts[: chips // 2 - 1 : -1])
    sent = high[0].astype(F32)
    for term in high[1:]:
        sent += term.astype(F32)
    mirrored = exchange(sent.astype(BF16), "seq", CORES * (chips - 1))
    return chip_reduce(parts[: chips // 2]) + [mirrored]


def device_sum(array):
    for axis in ("seq", "img"):
        apart = 1
        while apart < lax.axis_size(axis):
            array = array + exchange(array, axis, apart)
            apart *= 2
    return array


def chunk_bounds(half):
    return ((0, half),)


def local(query_proj, key_proj, value_proj, merge_cells, unmerge, grad_out, query_gain, key_gain):
    queries, key_rows, value_rows = query_proj[0], key_proj[0], value_proj[0]
    upstream = grad_out[0]
    tok, lanes = queries.shape
    half = lanes // CORES
    head_dim = query_gain.shape[0]
    cells = merge_cells.shape[1]
    chips = lax.axis_size("seq") // CORES
    bounds = chunk_bounds(half)
    widths = [stop - start for start, stop in bounds]
    query_row = jnp.tile(query_gain, TILE // head_dim)[None]
    key_row = jnp.tile(key_gain, TILE // head_dim)[None]

    merged = call(
        functools.partial(merge_kernel, head_dim, bounds),
        [((cells, 2 * width), BF16) for width in widths] * 2,
        [key_rows, value_rows, merge_cells[0], key_row],
        [((CORES, cells, 2 * width), BF16) for width in widths],
    )
    gathered = []
    for own, sent in zip(merged[: len(bounds)], merged[len(bounds) :]):
        block = jnp.concatenate([own, exchange(sent, "seq", 1)], axis=0)
        gathered.append(chip_gather(block, chips))

    (packed,) = call(pack_kernel, [((tok, lanes), BF16)], [queries, upstream])
    arrived = exchange(packed, "seq", 1)
    normed, both_upstream = call(
        functools.partial(query_kernel, head_dim),
        [((CORES * tok, half), BF16)] * 2,
        [queries, upstream, arrived, query_row],
    )

    group = min(chips, 4)
    attended, grads, key_sums, terms = [], [], [], []
    for (start, stop), width, blocks in zip(bounds, widths, gathered):
        results = call(
            functools.partial(attend_kernel, head_dim, start, chips, group),
            [
                ((CORES * tok, width), BF16),
                ((CORES * tok, width), F32),
                ((1, TILE), F32),
                ((CORES * cells, 2 * width), F32),
            ]
            + [((CORES * cells, 2 * width), BF16)] * (chips - 1),
            [normed, both_upstream, key_row] + blocks,
        )
        attended.append(results[0])
        grads.append(results[1])
        key_sums.append(results[2])
        terms.append(chip_reduce(results[3:]))

    own_part, sent_part, gain_sums = call(
        functools.partial(query_back_kernel, head_dim, bounds),
        [((tok, lanes), BF16)] * 2 + [((1, 2 * head_dim), F32)],
        [queries, arrived, query_row] + attended + grads + key_sums,
    )
    attended_all, grad_query = call(
        place_kernel,
        [((tok, lanes), BF16)] * 2,
        [own_part, exchange(sent_part, "seq", 1)],
    )
    gain_total = device_sum(gain_sums)[0]

    returned = []
    for chunk in terms:
        sent = chunk[0][cells:].astype(F32)
        for term in chunk[1:]:
            sent = sent + term[cells:].astype(F32)
        returned.append(exchange(sent, "seq", 1))
    grad_key, grad_value = call(
        functools.partial(key_back_kernel, head_dim, bounds, len(terms[0])),
        [((tok, lanes), BF16)] * 2,
        [key_rows, unmerge, key_row] + [term for chunk in terms for term in chunk] + returned,
        [((CORES, cells, 2 * width), F32) for width in widths],
    )
    return (
        attended_all[None],
        grad_query[None],
        grad_key[None],
        grad_value[None],
        gain_total[:head_dim],
        gain_total[head_dim:],
    )


def solution(mesh):
    rows = P("img", "seq", None)
    return jax.shard_map(
        local,
        mesh=mesh,
        in_specs=(rows, rows, rows, rows, P("img", "seq"), rows, P(), P()),
        out_specs=(rows, rows, rows, rows, P(), P()),
        check_vma=False,
    )
```

```python
import functools
import math

import jax
import jax.numpy as jnp
from jax import lax
from jax.experimental import pallas as pl
from jax.experimental.pallas import tpu as pltpu
from jax.sharding import PartitionSpec as P

EPSILON = 1e-06
TILE = 128
CORES = 2
BF16 = jnp.bfloat16
F32 = jnp.float32
VMEM_BYTES = 40 * 1024 * 1024
ALL_VMEM_BYTES = 62 * 1024 * 1024


def call(kernel, out_shapes, inputs, scratch=(), far_in=0, far_out=0, copies=0, aliases=None, vmem=VMEM_BYTES, micros=1.0):
    near, far = pl.BlockSpec(memory_space=pltpu.VMEM), pl.BlockSpec(memory_space=pltpu.HBM)
    buffers = [pltpu.VMEM(shape, kind) for shape, kind in scratch]
    if copies:
        buffers.append(pltpu.SemaphoreType.DMA((copies,)))
    return pl.pallas_call(
        kernel,
        out_shape=[jax.ShapeDtypeStruct(shape, kind) for shape, kind in out_shapes],
        in_specs=[far] * far_in + [near] * (len(inputs) - far_in),
        out_specs=[far] * far_out + [near] * (len(out_shapes) - far_out),
        scratch_shapes=buffers,
        input_output_aliases=aliases or {},
        cost_estimate=pl.CostEstimate(
            flops=int(micros * 1e9), bytes_accessed=int(micros * 2e6), transcendentals=0
        ),
        compiler_params=pltpu.CompilerParams(vmem_limit_bytes=vmem),
    )(*inputs)


def core_side():
    return lax.rem(lax.axis_index("seq"), CORES)


def lanes_at(index, width=TILE):
    return pl.ds(pl.multiple_of(index * TILE, TILE), width)


def pieces(width):
    return [(at, min(at + 2 * TILE, width)) for at in range(0, width, 2 * TILE)]


def dot(left, right, contract=((1,), (0,))):
    return lax.dot_general(left, right, (contract, ((), ())), preferred_element_type=F32)


def halves(array):
    high = array.astype(BF16)
    return high, (array - high.astype(F32)).astype(BF16)


def over_heads(array, head_dim, finish):
    head = lax.broadcasted_iota(jnp.int32, (1, TILE), 1) // head_dim
    tiles = []
    for at in range(0, array.shape[1], TILE):
        tile = array[:, at : at + TILE]
        result = None
        for index in range(TILE // head_dim):
            total = jnp.sum(jnp.where(head == index, tile, 0.0), axis=1, keepdims=True)
            value = finish(total * (1.0 / head_dim))
            result = value if result is None else jnp.where(head == index, value, result)
        tiles.append(jnp.broadcast_to(result, tile.shape))
    return jnp.concatenate(tiles, axis=1)


def unit_rows(array, head_dim):
    scale = over_heads(array * array, head_dim, lambda mean: lax.rsqrt(mean + EPSILON))
    return array * scale, scale


def norm_back(grad_normed, unit_vals, scale, gain_row, head_dim):
    grad_unit = grad_normed * gain_row
    mean_inner = over_heads(grad_unit * unit_vals, head_dim, lambda mean: mean)
    return scale * (grad_unit - unit_vals * mean_inner)


def gain_lanes(gain_ref, width):
    row = gain_ref[...]
    return jnp.concatenate([row] * (width // row.shape[1]), axis=1)


def merge_kernel(head_dim, bounds, key_ref, value_ref, cells_ref, gain_ref, *refs):
    count = len(bounds)
    own_refs, send_refs = refs[:count], refs[count : 2 * count]
    key_buf, value_buf, cells_buf, gain_buf, copied = refs[2 * count :]
    tok, lanes = key_buf.shape
    half = lanes // CORES
    cells = cells_ref.shape[1]
    side = core_side()
    small = [
        pltpu.make_async_copy(cells_ref, cells_buf, copied.at[0]),
        pltpu.make_async_copy(gain_ref, gain_buf, copied.at[1]),
    ]
    for move in small:
        move.start()
    spans = [
        (other, chunk, start, stop, start + at, start + to)
        for other in (1, 0)
        for chunk, (start, stop) in enumerate(bounds)
        for at, to in pieces(stop - start)
    ]
    moves = []
    for index, (other, _, _, _, at, to) in enumerate(spans):
        source = lanes_at((1 - side if other else side) * (half // TILE) + at // TILE, to - at)
        here = slice(other * half + at, other * half + to)
        for which, (far, near) in enumerate(((key_ref, key_buf), (value_ref, value_buf))):
            move = pltpu.make_async_copy(
                far.at[:, source], near.at[:, here], copied.at[2 + 2 * index + which]
            )
            move.start()
            moves.append(move)
    for move in small:
        move.wait()
    listed = lax.rem(cells_buf[...], tok)
    ids = lax.broadcasted_iota(jnp.int32, (tok, cells), 0)
    member = sum((listed[j : j + 1] == ids).astype(F32) for j in range(cells_ref.shape[0]))
    member = member.T.astype(BF16)
    twice = jnp.concatenate([member, member], axis=1)
    for index, (other, chunk, start, stop, at, to) in enumerate(spans):
        here = slice(other * half + at, other * half + to)
        out_ref = (send_refs if other else own_refs)[chunk]
        if index % (len(spans) // CORES) == 0:
            for move in moves[2 * index : 2 * index + 2 * len(spans) // CORES]:
                move.wait()
        unit_vals, _ = unit_rows(key_buf[:, here].astype(F32), head_dim)
        keys = dot(twice, jnp.concatenate(halves(unit_vals), axis=0))
        keys *= gain_lanes(gain_buf, to - at) * 0.25
        out_ref[:, at - start : to - start] = keys.astype(BF16)
        values = dot(member, value_buf[:, here]) * 0.25
        out_ref[:, stop - 2 * start + at : stop - 2 * start + to] = values.astype(BF16)


def pack_kernel(query_ref, upstream_ref, send_ref, copied):
    half = query_ref.shape[1] // CORES
    source = lanes_at((1 - core_side()) * (half // TILE), half)
    moves = [
        pltpu.make_async_copy(query_ref.at[:, source], send_ref.at[:, :half], copied.at[0]),
        pltpu.make_async_copy(upstream_ref.at[:, source], send_ref.at[:, half:], copied.at[1]),
    ]
    for move in moves:
        move.start()
    for move in moves:
        move.wait()


def query_kernel(
    head_dim, query_ref, upstream_ref, arrived_ref, gain_ref, raw_ref, out_ref, grad_ref, copied
):
    tok, lanes = query_ref.shape
    half = lanes // CORES
    source = lanes_at(core_side() * (half // TILE), half)
    moves = [
        pltpu.make_async_copy(query_ref.at[:, source], raw_ref.at[:tok], copied.at[0]),
        pltpu.make_async_copy(upstream_ref.at[:, source], grad_ref.at[:tok], copied.at[1]),
    ]
    for move in moves:
        move.start()
    raw_ref[tok:] = arrived_ref[:, :half]
    grad_ref[tok:] = arrived_ref[:, half:]
    moves[0].wait()
    for at, to in pieces(half):
        unit_vals, _ = unit_rows(raw_ref[:, at:to].astype(F32), head_dim)
        out_ref[:, at:to] = (unit_vals * gain_lanes(gain_ref, to - at)).astype(BF16)
    moves[1].wait()


def attend_kernel(head_dim, start, blocks, group, *refs):
    query_ref, upstream_ref, query_gain_ref, key_gain_ref = refs[:4]
    block_refs = refs[4 : 4 + blocks]
    attended_ref, grad_ref, gain_out_ref = refs[4 + blocks : 7 + blocks]
    part_refs = refs[7 + blocks :]
    rows = query_ref.shape[0]
    block_rows, width = block_refs[0].shape
    width = width // 2
    per = TILE // head_dim
    cells = group * block_rows
    scale = head_dim**-0.5
    exponent = scale * math.log2(math.e)
    lane_head = lax.broadcasted_iota(jnp.int32, (1, TILE), 1) // head_dim
    cell_heads = lax.broadcasted_iota(jnp.int32, (cells, TILE), 1) // head_dim
    masks = [(cell_heads == head).astype(F32).astype(BF16) for head in range(per)]

    def spread(array):
        return jnp.concatenate([array * mask for mask in masks], axis=0)

    def by_lane(parts):
        result = parts[0]
        for head in range(1, per):
            result = jnp.where(lane_head == head, parts[head], result)
        return result

    def folded(array):
        return by_lane([array[head * cells : (head + 1) * cells] for head in range(per)])

    def one_tile(tile, sums):
        query_sum, key_sum = sums
        lane = lanes_at(tile)
        value_lane = lanes_at(width // TILE + tile)
        source = lanes_at(start // TILE + tile)
        queries = query_ref[:, source]
        upstream = upstream_ref[:, source]
        weighted = jnp.zeros((rows, TILE), F32)
        totals = [jnp.zeros((rows, 1), F32) for _ in range(per)]
        held = []
        for first in range(0, blocks, group):
            members = block_refs[first : first + group]
            keys = jnp.concatenate([ref[:, lane] for ref in members], axis=0)
            spread_keys = spread(keys)
            spread_values = spread(
                jnp.concatenate([ref[:, value_lane] for ref in members], axis=0)
            )
            scores = dot(queries, spread_keys, ((1,), (1,)))
            exp_scores = jnp.exp2(scores * exponent)
            weighted += dot(exp_scores.astype(BF16), spread_values)
            exp_parts = [exp_scores[:, h * cells : (h + 1) * cells] for h in range(per)]
            totals = [
                total + jnp.sum(part, axis=1, keepdims=True)
                for total, part in zip(totals, exp_parts)
            ]
            held.append((keys, spread_keys, spread_values, exp_parts))
        inverses = [1.0 / total for total in totals]
        attended = (weighted * by_lane(inverses)).astype(BF16)
        attended_ref[:, lane] = attended
        products = upstream.astype(F32) * attended.astype(F32)
        inners = [
            jnp.sum(jnp.where(lane_head == h, products, 0.0), axis=1, keepdims=True)
            for h in range(per)
        ]
        grad_queries = jnp.zeros((rows, TILE), F32)
        for index, (keys, spread_keys, spread_values, exp_parts) in enumerate(held):
            grad_weights = dot(upstream, spread_values, ((1,), (1,)))
            attention = [part * inverse for part, inverse in zip(exp_parts, inverses)]
            grad_scores = jnp.concatenate(
                [
                    (attention[h] * (grad_weights[:, h * cells : (h + 1) * cells] - inners[h]))
                    .astype(BF16)
                    for h in range(per)
                ],
                axis=1,
            )
            attention_bf = jnp.concatenate([part.astype(BF16) for part in attention], axis=1)
            grad_queries += dot(grad_scores, spread_keys)
            grad_keys = folded(dot(grad_scores, queries, ((0,), (0,)))) * scale
            grad_values = folded(dot(attention_bf, upstream, ((0,), (0,))))
            key_sum += jnp.sum(grad_keys * keys.astype(F32), axis=0, keepdims=True)
            for member in range(group):
                ref = part_refs[index * group + member]
                here = slice(member * block_rows, (member + 1) * block_rows)
                ref[:, lane] = grad_keys[here].astype(ref.dtype)
                ref[:, value_lane] = grad_values[here].astype(ref.dtype)
        grad_queries *= scale
        grad_ref[:, lane] = grad_queries
        query_sum += jnp.sum(grad_queries * queries.astype(F32), axis=0, keepdims=True)
        return query_sum, key_sum

    sums = (jnp.zeros((1, TILE), F32), jnp.zeros((1, TILE), F32))
    if blocks == group:
        for tile in range(width // TILE):
            sums = one_tile(tile, sums)
    else:
        sums = lax.fori_loop(0, width // TILE, one_tile, sums)

    def per_channel(row):
        return sum(row[:, at : at + head_dim] for at in range(0, TILE, head_dim))

    gain_out_ref[...] = jnp.concatenate(
        [
            per_channel(sums[0]) / query_gain_ref[...],
            per_channel(sums[1]) / key_gain_ref[...],
        ],
        axis=1,
    )


def query_back_kernel(head_dim, bounds, raw_ref, gain_ref, *refs):
    count = len(bounds)
    attended_refs, grad_refs = refs[:count], refs[count : 2 * count]
    attended_out, grad_out, send_ref, attended_buf, grad_buf, copied = refs[2 * count :]
    tok, half = attended_buf.shape
    for (start, stop), attended_ref, grad_ref in zip(bounds, attended_refs, grad_refs):
        attended_buf[:, start:stop] = attended_ref[:tok]
        send_ref[:, start:stop] = attended_ref[tok:]
        for at, to in pieces(stop - start):
            lane = slice(start + at, start + to)
            unit_vals, scale = unit_rows(raw_ref[:, lane].astype(F32), head_dim)
            grads = norm_back(
                grad_ref[:, at:to], unit_vals, scale, gain_lanes(gain_ref, to - at), head_dim
            ).astype(BF16)
            grad_buf[:, lane] = grads[:tok]
            send_ref[:, half + start + at : half + start + to] = grads[tok:]
    place = lanes_at(core_side() * (half // TILE), half)
    moves = [
        pltpu.make_async_copy(attended_buf, attended_out.at[:, place], copied.at[0]),
        pltpu.make_async_copy(grad_buf, grad_out.at[:, place], copied.at[1]),
    ]
    for move in moves:
        move.start()
    for move in moves:
        move.wait()


def place_kernel(attended_in, grad_in, arrived_ref, attended_out, grad_out, copied):
    half = arrived_ref.shape[1] // 2
    place = lanes_at((1 - core_side()) * (half // TILE), half)
    moves = [
        pltpu.make_async_copy(arrived_ref.at[:, :half], attended_out.at[:, place], copied.at[0]),
        pltpu.make_async_copy(arrived_ref.at[:, half:], grad_out.at[:, place], copied.at[1]),
    ]
    for move in moves:
        move.start()
    for move in moves:
        move.wait()


def key_back_kernel(bounds, terms, other, *refs):
    count = len(bounds)
    if other:
        refs = refs[2:]
    key_ref, unmerge_ref, gain_ref = refs[:3]
    term_refs = [refs[3 + chunk * terms : 3 + (chunk + 1) * terms] for chunk in range(count)]
    grad_key_out, grad_value_out, grad_key_buf, grad_value_buf, copied = refs[3 + count * terms :]
    tok, half = grad_key_buf.shape
    cells = term_refs[0][0].shape[0] // (1 if other else CORES)
    side = core_side()
    first = (1 - side if other else side) * (half // TILE)
    owner = lax.rem(unmerge_ref[...], cells)
    table = (lax.broadcasted_iota(jnp.int32, (cells, tok), 0) == owner).astype(F32)
    table = table.T.astype(BF16)
    twice = jnp.concatenate([table, table], axis=1)

    def spread(chunk, at, to):
        result = term_refs[chunk][0][:cells, at:to].astype(F32)
        for ref in term_refs[chunk][1:]:
            result += ref[:cells, at:to].astype(F32)
        return dot(twice, jnp.concatenate(halves(result), axis=0)) * 0.25

    spans = [
        (chunk, start, stop, start + at, start + to)
        for chunk, (start, stop) in enumerate(bounds)
        for at, to in pieces(stop - start)
    ]
    moves = []

    def send(index, buf, out):
        move = pltpu.make_async_copy(buf, out.at[:, lanes_at(first, half)], copied.at[index])
        move.start()
        moves.append(move)

    for chunk, start, stop, at, to in spans:
        grad_value_buf[:, at:to] = spread(chunk, stop - 2 * start + at, stop - 2 * start + to).astype(
            BF16
        )
    send(0, grad_value_buf, grad_value_out)
    for chunk, start, stop, at, to in spans:
        keys = key_ref[:, lanes_at(first + at // TILE, to - at)].astype(F32)
        unit_vals, scale = unit_rows(keys, gain_ref.shape[1])
        grad_key_buf[:, at:to] = norm_back(
            spread(chunk, at - start, to - start),
            unit_vals,
            scale,
            gain_lanes(gain_ref, to - at),
            gain_ref.shape[1],
        ).astype(BF16)
    send(1, grad_key_buf, grad_key_out)
    for move in moves:
        move.wait()


def exchange(array, axis, apart):
    return lax.ppermute(array, axis, [(i, i ^ apart) for i in range(lax.axis_size(axis))])


def chip_gather(block, chips):
    if chips == 1:
        return [block]
    mirrored = exchange(block, "seq", CORES * (chips - 1))
    return chip_gather(block, chips // 2) + chip_gather(mirrored, chips // 2)[::-1]


def chip_reduce(parts, between):
    chips = len(parts)
    if chips == 1:
        return [parts[0]]
    high = chip_reduce(parts[: chips // 2 - 1 : -1], between)
    if len(high) > 1:
        high = [high[0]] + between(high[1:])
    sent = high[0].astype(F32)
    for term in high[1:]:
        sent += term.astype(F32)
    mirrored = exchange(sent.astype(BF16), "seq", CORES * (chips - 1))
    return chip_reduce(parts[: chips // 2], between) + [mirrored]


class Rest:
    def __init__(self, gains, chips):
        self.gains = gains
        self.steps = [("seq", 1)]
        images = lax.axis_size("img")
        image_steps = [("img", 1 << bit) for bit in range(images.bit_length() - 1)]
        chip_steps = [("seq", CORES << bit) for bit in range(chips.bit_length() - 1)]
        self.steps += chip_steps[:1] + image_steps + chip_steps[1:]

    def advance(self, count):
        for axis, apart in self.steps[:count]:
            self.gains = self.gains + exchange(self.gains, axis, apart)
        self.steps = self.steps[count:]


def chunk_bounds(half):
    return ((0, half),)


def local(query_proj, key_proj, value_proj, merge_cells, unmerge, grad_out, query_gain, key_gain):
    queries, key_rows, value_rows = query_proj[0], key_proj[0], value_proj[0]
    upstream = grad_out[0]
    tok, lanes = queries.shape
    half = lanes // CORES
    head_dim = query_gain.shape[0]
    cells = merge_cells.shape[1]
    chips = lax.axis_size("seq") // CORES
    bounds = chunk_bounds(half)
    widths = [stop - start for start, stop in bounds]
    query_row, key_row = query_gain[None], key_gain[None]

    merged = call(
        functools.partial(merge_kernel, head_dim, bounds),
        [((cells, 2 * width), BF16) for width in widths] * 2,
        [key_rows, value_rows, merge_cells[0].T, key_row],
        scratch=[((tok, lanes), BF16)] * 2
        + [(merge_cells.shape[:0:-1], jnp.int32), ((1, head_dim), F32)],
        far_in=4,
        copies=2 + 4 * sum(len(pieces(width)) for width in widths),
        vmem=ALL_VMEM_BYTES,
    )
    gathered = []
    for own, sent in zip(merged[: len(bounds)], merged[len(bounds) :]):
        block = jnp.concatenate([own, exchange(sent, "seq", 1)], axis=0)
        gathered.append(chip_gather(block, chips))

    (packed,) = call(
        pack_kernel, [((tok, lanes), BF16)], [queries, upstream], far_in=2, copies=2
    )
    raw, normed, both_upstream = call(
        functools.partial(query_kernel, head_dim),
        [((CORES * tok, half), BF16)] * 3,
        [queries, upstream, exchange(packed, "seq", 1), query_row],
        far_in=2,
        copies=2,
    )

    group = min(chips, 4)
    results = [
        call(
            functools.partial(attend_kernel, head_dim, start, chips, group),
            [
                ((CORES * tok, width), BF16),
                ((CORES * tok, width), F32),
                ((1, 2 * head_dim), F32),
                ((CORES * cells, 2 * width), F32),
            ]
            + [((CORES * cells, 2 * width), BF16)] * (chips - 1),
            [normed, both_upstream, query_row, key_row] + blocks,
            micros=3.5 * width / half,
        )
        for (start, stop), width, blocks in zip(bounds, widths, gathered)
    ]
    attended = [result[0] for result in results]
    grads = [result[1] for result in results]
    rest = Rest(sum(result[2] for result in results), chips)
    placed = []

    def between(arrays):
        if not placed:
            rest.advance(2)
            placed.extend(
                call(
                    functools.partial(query_back_kernel, head_dim, bounds),
                    [((tok, lanes), BF16)] * 3,
                    [raw, query_row] + attended + grads,
                    scratch=[((tok, half), BF16)] * 2,
                    far_out=2,
                    copies=2,
                )
            )
            arrays, rest.gains, placed[2] = lax.optimization_barrier(
                (arrays, rest.gains, placed[2])
            )
        return arrays

    terms = [chip_reduce(result[3:], between) for result in results]
    between([])
    rest.advance(2)
    attended_all, grad_query = call(
        place_kernel,
        [((tok, lanes), BF16)] * 2,
        [placed[0], placed[1], exchange(placed[2], "seq", 1)],
        far_in=2,
        far_out=2,
        copies=2,
        aliases={0: 0, 1: 1},
    )
    terms, rest.gains, attended_all, grad_query = lax.optimization_barrier(
        (terms, rest.gains, attended_all, grad_query)
    )
    rest.advance(len(rest.steps))
    gain_total = rest.gains[0]

    returned = []
    for chunk in terms:
        sent = chunk[0][cells:].astype(F32)
        for term in chunk[1:]:
            sent = sent + term[cells:].astype(F32)
        returned.append(exchange(sent, "seq", 1))

    def key_grads(other, outputs, sources, count):
        return call(
            functools.partial(key_back_kernel, bounds, count, other),
            [((tok, lanes), BF16)] * 2,
            outputs + [key_rows, unmerge, key_row] + sources,
            scratch=[((tok, half), BF16)] * 2,
            far_in=len(outputs),
            far_out=2,
            copies=2,
            aliases={0: 0, 1: 1} if other else None,
            micros=1.2,
        )

    partial_grads = key_grads(False, [], [term for chunk in terms for term in chunk], len(terms[0]))
    grad_key, grad_value = key_grads(True, list(partial_grads), returned, 1)
    return (
        attended_all[None],
        grad_query[None],
        grad_key[None],
        grad_value[None],
        gain_total[:head_dim],
        gain_total[head_dim:],
    )


def solution(mesh):
    rows = P("img", "seq", None)
    return jax.shard_map(
        local,
        mesh=mesh,
        in_specs=(rows, rows, rows, rows, P("img", "seq"), rows, P(), P()),
        out_specs=(rows, rows, rows, rows, P(), P()),
        check_vma=False,
    )
```

```python
import functools
import math

import jax
import jax.numpy as jnp
from jax import lax
from jax.experimental import pallas as pl
from jax.experimental.pallas import tpu as pltpu
from jax.sharding import PartitionSpec as P

EPSILON = 1e-06
TILE = 128
CORES = 2
BF16 = jnp.bfloat16
F32 = jnp.float32
VMEM_BYTES = 40 * 1024 * 1024
ALL_VMEM_BYTES = 62 * 1024 * 1024


def call(kernel, out_shapes, inputs, scratch=(), far_in=0, far_out=0, copies=0, aliases=None, vmem=VMEM_BYTES, micros=1.0):
    near, far = pl.BlockSpec(memory_space=pltpu.VMEM), pl.BlockSpec(memory_space=pltpu.HBM)
    buffers = [pltpu.VMEM(shape, kind) for shape, kind in scratch]
    if copies:
        buffers.append(pltpu.SemaphoreType.DMA((copies,)))
    return pl.pallas_call(
        kernel,
        out_shape=[jax.ShapeDtypeStruct(shape, kind) for shape, kind in out_shapes],
        in_specs=[far] * far_in + [near] * (len(inputs) - far_in),
        out_specs=[far] * far_out + [near] * (len(out_shapes) - far_out),
        scratch_shapes=buffers,
        input_output_aliases=aliases or {},
        cost_estimate=pl.CostEstimate(
            flops=int(micros * 1e9), bytes_accessed=int(micros * 2e6), transcendentals=0
        ),
        compiler_params=pltpu.CompilerParams(vmem_limit_bytes=vmem),
    )(*inputs)


def core_side():
    return lax.rem(lax.axis_index("seq"), CORES)


def lanes_at(index, width=TILE):
    return pl.ds(pl.multiple_of(index * TILE, TILE), width)


def pieces(width):
    return [(at, min(at + 2 * TILE, width)) for at in range(0, width, 2 * TILE)]


def dot(left, right, contract=((1,), (0,))):
    return lax.dot_general(left, right, (contract, ((), ())), preferred_element_type=F32)


def halves(array):
    high = array.astype(BF16)
    return high, (array - high.astype(F32)).astype(BF16)


def over_heads(array, head_dim, finish):
    head = lax.broadcasted_iota(jnp.int32, (1, TILE), 1) // head_dim
    tiles = []
    for at in range(0, array.shape[1], TILE):
        tile = array[:, at : at + TILE]
        result = None
        for index in range(TILE // head_dim):
            total = jnp.sum(jnp.where(head == index, tile, 0.0), axis=1, keepdims=True)
            value = finish(total * (1.0 / head_dim))
            result = value if result is None else jnp.where(head == index, value, result)
        tiles.append(jnp.broadcast_to(result, tile.shape))
    return jnp.concatenate(tiles, axis=1)


def unit_rows(array, head_dim):
    scale = over_heads(array * array, head_dim, lambda mean: lax.rsqrt(mean + EPSILON))
    return array * scale, scale


def norm_back(grad_normed, unit_vals, scale, gain_row, head_dim):
    grad_unit = grad_normed * gain_row
    mean_inner = over_heads(grad_unit * unit_vals, head_dim, lambda mean: mean)
    return scale * (grad_unit - unit_vals * mean_inner)


def gain_lanes(gain_ref, width):
    row = gain_ref[...]
    return jnp.concatenate([row] * (width // row.shape[1]), axis=1)


def merge_kernel(head_dim, bounds, key_ref, value_ref, cells_ref, gain_ref, *refs):
    count = len(bounds)
    own_refs, send_refs = refs[:count], refs[count : 2 * count]
    key_buf, value_buf, cells_buf, gain_buf, copied = refs[2 * count :]
    tok, lanes = key_buf.shape
    half = lanes // CORES
    cells = cells_ref.shape[1]
    side = core_side()
    small = [
        pltpu.make_async_copy(cells_ref, cells_buf, copied.at[0]),
        pltpu.make_async_copy(gain_ref, gain_buf, copied.at[1]),
    ]
    for move in small:
        move.start()
    spans = [
        (other, chunk, start, stop, start + at, start + to)
        for other in (1, 0)
        for chunk, (start, stop) in enumerate(bounds)
        for at, to in pieces(stop - start)
    ]
    moves = []
    for index, (other, _, _, _, at, to) in enumerate(spans):
        source = lanes_at((1 - side if other else side) * (half // TILE) + at // TILE, to - at)
        here = slice(other * half + at, other * half + to)
        for which, (far, near) in enumerate(((key_ref, key_buf), (value_ref, value_buf))):
            move = pltpu.make_async_copy(
                far.at[:, source], near.at[:, here], copied.at[2 + 2 * index + which]
            )
            move.start()
            moves.append(move)
    for move in small:
        move.wait()
    listed = lax.rem(cells_buf[...], tok)
    ids = lax.broadcasted_iota(jnp.int32, (tok, cells), 0)
    member = sum((listed[j : j + 1] == ids).astype(F32) for j in range(cells_ref.shape[0]))
    member = member.T.astype(BF16)
    twice = jnp.concatenate([member, member], axis=1)
    for index, (other, chunk, start, stop, at, to) in enumerate(spans):
        here = slice(other * half + at, other * half + to)
        out_ref = (send_refs if other else own_refs)[chunk]
        if index % (len(spans) // CORES) == 0:
            for move in moves[2 * index : 2 * index + 2 * len(spans) // CORES]:
                move.wait()
        unit_vals, _ = unit_rows(key_buf[:, here].astype(F32), head_dim)
        keys = dot(twice, jnp.concatenate(halves(unit_vals), axis=0))
        keys *= gain_lanes(gain_buf, to - at) * 0.25
        out_ref[:, at - start : to - start] = keys.astype(BF16)
        values = dot(member, value_buf[:, here]) * 0.25
        out_ref[:, stop - 2 * start + at : stop - 2 * start + to] = values.astype(BF16)


def pack_kernel(query_ref, upstream_ref, send_ref, copied):
    half = query_ref.shape[1] // CORES
    source = lanes_at((1 - core_side()) * (half // TILE), half)
    moves = [
        pltpu.make_async_copy(query_ref.at[:, source], send_ref.at[:, :half], copied.at[0]),
        pltpu.make_async_copy(upstream_ref.at[:, source], send_ref.at[:, half:], copied.at[1]),
    ]
    for move in moves:
        move.start()
    for move in moves:
        move.wait()


def query_kernel(
    head_dim, query_ref, upstream_ref, arrived_ref, gain_ref, unit_ref, scale_ref, *refs
):
    out_ref, grad_ref, copied = refs
    tok, lanes = query_ref.shape
    half = lanes // CORES
    side = core_side()
    source = lanes_at(side * (half // TILE), half)
    move = pltpu.make_async_copy(upstream_ref.at[:, source], grad_ref.at[:tok], copied.at[0])
    move.start()
    grad_ref[tok:] = arrived_ref[:, half:]
    for at, to in pieces(half):
        for row, queries in (
            (0, query_ref[:, lanes_at(side * (half // TILE) + at // TILE, to - at)]),
            (tok, arrived_ref[:, at:to]),
        ):
            here = slice(row, row + tok)
            unit_vals, scale = unit_rows(queries.astype(F32), head_dim)
            unit_ref[here, at:to] = unit_vals
            scale_ref[here, at:to] = scale
            out_ref[here, at:to] = (unit_vals * gain_lanes(gain_ref, to - at)).astype(BF16)
    move.wait()


def key_kernel(head_dim, key_ref, unmerge_ref, gain_ref, unit_ref, scale_ref, table_ref, row_ref):
    tok = key_ref.shape[0]
    cells = table_ref.shape[1] // 2
    owner = lax.rem(unmerge_ref[...], cells)
    table = (lax.broadcasted_iota(jnp.int32, (cells, tok), 0) == owner).astype(F32) * 0.25
    table = table.T.astype(BF16)
    table_ref[...] = jnp.concatenate([table, table], axis=1)
    row_ref[...] = gain_lanes(gain_ref, row_ref.shape[1])
    for at, to in pieces(key_ref.shape[1]):
        unit_vals, scale = unit_rows(key_ref[:, at:to].astype(F32), head_dim)
        unit_ref[:, at:to] = unit_vals
        scale_ref[:, at:to] = scale


def attend_kernel(head_dim, start, blocks, group, *refs):
    query_ref, upstream_ref = refs[:2]
    block_refs = refs[2 : 2 + blocks]
    attended_ref, grad_ref, gain_out_ref = refs[2 + blocks : 5 + blocks]
    part_refs = refs[5 + blocks :]
    rows = query_ref.shape[0]
    block_rows, width = block_refs[0].shape
    width = width // 2
    per = TILE // head_dim
    cells = group * block_rows
    scale = head_dim**-0.5
    exponent = scale * math.log2(math.e)
    lane_head = lax.broadcasted_iota(jnp.int32, (1, TILE), 1) // head_dim
    cell_heads = lax.broadcasted_iota(jnp.int32, (cells, TILE), 1) // head_dim
    masks = [(cell_heads == head).astype(F32).astype(BF16) for head in range(per)]

    def spread(array):
        return jnp.concatenate([array * mask for mask in masks], axis=0)

    def by_lane(parts):
        result = parts[0]
        for head in range(1, per):
            result = jnp.where(lane_head == head, parts[head], result)
        return result

    def folded(array):
        return by_lane([array[head * cells : (head + 1) * cells] for head in range(per)])

    def one_tile(tile, sums):
        query_sum, key_sum = sums
        lane = lanes_at(tile)
        value_lane = lanes_at(width // TILE + tile)
        source = lanes_at(start // TILE + tile)
        queries = query_ref[:, source]
        upstream = upstream_ref[:, source]
        weighted = jnp.zeros((rows, TILE), F32)
        totals = [jnp.zeros((rows, 1), F32) for _ in range(per)]
        held = []
        for first in range(0, blocks, group):
            members = block_refs[first : first + group]
            keys = jnp.concatenate([ref[:, lane] for ref in members], axis=0)
            spread_keys = spread(keys)
            spread_values = spread(
                jnp.concatenate([ref[:, value_lane] for ref in members], axis=0)
            )
            scores = dot(queries, spread_keys, ((1,), (1,)))
            exp_scores = jnp.exp2(scores * exponent)
            weighted += dot(exp_scores.astype(BF16), spread_values)
            exp_parts = [exp_scores[:, h * cells : (h + 1) * cells] for h in range(per)]
            totals = [
                total + jnp.sum(part, axis=1, keepdims=True)
                for total, part in zip(totals, exp_parts)
            ]
            held.append((keys, spread_keys, spread_values, exp_parts))
        inverses = [1.0 / total for total in totals]
        attended = (weighted * by_lane(inverses)).astype(BF16)
        attended_ref[:, lane] = attended
        products = upstream.astype(F32) * attended.astype(F32)
        inners = [
            jnp.sum(jnp.where(lane_head == h, products, 0.0), axis=1, keepdims=True)
            for h in range(per)
        ]
        grad_queries = jnp.zeros((rows, TILE), F32)
        for index, (keys, spread_keys, spread_values, exp_parts) in enumerate(held):
            grad_weights = dot(upstream, spread_values, ((1,), (1,)))
            attention = [part * inverse for part, inverse in zip(exp_parts, inverses)]
            grad_scores = jnp.concatenate(
                [
                    (attention[h] * (grad_weights[:, h * cells : (h + 1) * cells] - inners[h]))
                    .astype(BF16)
                    for h in range(per)
                ],
                axis=1,
            )
            attention_bf = jnp.concatenate([part.astype(BF16) for part in attention], axis=1)
            grad_queries += dot(grad_scores, spread_keys)
            grad_keys = folded(dot(grad_scores, queries, ((0,), (0,)))) * scale
            grad_values = folded(dot(attention_bf, upstream, ((0,), (0,))))
            key_sum += jnp.sum(grad_keys * keys.astype(F32), axis=0, keepdims=True)
            for member in range(group):
                ref = part_refs[index * group + member]
                here = slice(member * block_rows, (member + 1) * block_rows)
                ref[:, lane] = grad_keys[here].astype(ref.dtype)
                ref[:, value_lane] = grad_values[here].astype(ref.dtype)
        grad_queries *= scale
        grad_ref[:, lane] = grad_queries
        query_sum += jnp.sum(grad_queries * queries.astype(F32), axis=0, keepdims=True)
        return query_sum, key_sum

    sums = (jnp.zeros((1, TILE), F32), jnp.zeros((1, TILE), F32))
    if blocks == group:
        for tile in range(width // TILE):
            sums = one_tile(tile, sums)
    else:
        sums = lax.fori_loop(0, width // TILE, one_tile, sums)

    def per_channel(row):
        return sum(row[:, at : at + head_dim] for at in range(0, TILE, head_dim))

    gain_out_ref[...] = jnp.concatenate([per_channel(row) for row in sums], axis=1)


def query_back_kernel(head_dim, bounds, unit_ref, scale_ref, gain_ref, *refs):
    count = len(bounds)
    attended_refs, grad_refs = refs[:count], refs[count : 2 * count]
    attended_out, grad_out, send_ref, attended_buf, grad_buf, copied = refs[2 * count :]
    tok, half = attended_buf.shape
    for (start, stop), attended_ref, grad_ref in zip(bounds, attended_refs, grad_refs):
        attended_buf[:, start:stop] = attended_ref[:tok]
        send_ref[:, start:stop] = attended_ref[tok:]
        for at, to in pieces(stop - start):
            lane = slice(start + at, start + to)
            grads = norm_back(
                grad_ref[:, at:to],
                unit_ref[:, lane],
                scale_ref[:, lane],
                gain_lanes(gain_ref, to - at),
                head_dim,
            ).astype(BF16)
            grad_buf[:, lane] = grads[:tok]
            send_ref[:, half + start + at : half + start + to] = grads[tok:]
    place = lanes_at(core_side() * (half // TILE), half)
    moves = [
        pltpu.make_async_copy(attended_buf, attended_out.at[:, place], copied.at[0]),
        pltpu.make_async_copy(grad_buf, grad_out.at[:, place], copied.at[1]),
    ]
    for move in moves:
        move.start()
    for move in moves:
        move.wait()


def key_back_kernel(head_dim, bounds, own_terms, other_terms, *refs):
    query_refs, refs = refs[2:3], refs[3:]
    unit_ref, scale_ref, table_ref, gain_ref = refs[:4]
    refs = refs[4:]
    sources = []
    for _ in bounds:
        sources.append((refs[:own_terms], refs[own_terms : own_terms + other_terms]))
        refs = refs[own_terms + other_terms :]
    grad_key_out, grad_value_out, *query_outs, grad_key_buf, grad_value_buf, copied = refs
    tok, half = grad_key_buf.shape[1:]
    cells = sources[0][1][0].shape[0]
    side = core_side()
    table = table_ref[...]

    def spread(chunk, other, at, to):
        total = added([ref[:cells, at:to] for ref in sources[chunk][other]])
        return dot(table, jnp.concatenate(halves(total), axis=0))

    spans = [
        (other, chunk, start, stop, start + at, start + to)
        for other in range(CORES)
        for chunk, (start, stop) in enumerate(bounds)
        for at, to in pieces(stop - start)
    ]
    moves = []

    def send(buf, out, other):
        place = lanes_at((1 - side if other else side) * (half // TILE), half)
        move = pltpu.make_async_copy(buf, out.at[:, place], copied.at[len(moves)])
        move.start()
        moves.append(move)

    for index, out in enumerate(query_outs):
        send(query_refs[0].at[:, index * half : (index + 1) * half], out, 1)
    for other, chunk, start, stop, at, to in spans:
        grad_value_buf[other, :, at:to] = spread(
            chunk, other, stop - 2 * start + at, stop - 2 * start + to
        ).astype(BF16)
    for other in range(CORES):
        send(grad_value_buf.at[other], grad_value_out, other)
    for other, chunk, start, stop, at, to in spans:
        first = (1 - side if other else side) * (half // TILE)
        lane = lanes_at(first + at // TILE, to - at)
        grad_key_buf[other, :, at:to] = norm_back(
            spread(chunk, other, at - start, to - start),
            unit_ref[:, lane],
            scale_ref[:, lane],
            gain_ref[:, : to - at],
            head_dim,
        ).astype(BF16)
        if to == half:
            send(grad_key_buf.at[other], grad_key_out, other)
    for move in moves:
        move.wait()


def exchange(array, axis, apart):
    return lax.ppermute(array, axis, [(i, i ^ apart) for i in range(lax.axis_size(axis))])


def chip_gather(block, chips):
    if chips == 1:
        return [block]
    mirrored = exchange(block, "seq", CORES * (chips - 1))
    return chip_gather(block, chips // 2) + chip_gather(mirrored, chips // 2)[::-1]


def chip_reduce(parts):
    chips = len(parts)
    if chips == 1:
        return [parts[0]]
    sent = added(chip_reduce(parts[: chips // 2 - 1 : -1])).astype(BF16)
    return chip_reduce(parts[: chips // 2]) + [exchange(sent, "seq", CORES * (chips - 1))]


def added(terms):
    total = terms[0].astype(F32)
    for term in terms[1:]:
        total += term.astype(F32)
    return total


class Rest:
    def __init__(self, gains, chips):
        self.gains = gains
        images = lax.axis_size("img")
        image_steps = [("img", 1 << bit) for bit in range(images.bit_length() - 1)]
        chip_steps = [("seq", CORES << bit) for bit in range(chips.bit_length() - 1)]
        self.table = {
            "c": [("seq", 1)],
            "y": image_steps[:1],
            "x": image_steps[1:],
            "z": chip_steps[:1],
            "w": chip_steps[1:],
            "D": [("seq", *(CORES * apart for apart in range(1, chips)))],
        }

    def advance(self, names):
        for name in names:
            for axis, *aparts in self.table[name]:
                arrived = [exchange(self.gains, axis, apart) for apart in aparts]
                self.gains = sum(arrived, self.gains)


OPT = dict(split=0, steps="cD|yx|", near=1, hb=0, sb=2, k4=0, kc=1.7, pc=1.0)


def chunk_bounds(half):
    return ((0, half),)


def local(query_proj, key_proj, value_proj, merge_cells, unmerge, grad_out, query_gain, key_gain):
    queries, key_rows, value_rows = query_proj[0], key_proj[0], value_proj[0]
    upstream = grad_out[0]
    tok, lanes = queries.shape
    half = lanes // CORES
    head_dim = query_gain.shape[0]
    cells = merge_cells.shape[1]
    chips = lax.axis_size("seq") // CORES
    bounds = chunk_bounds(half)
    widths = [stop - start for start, stop in bounds]
    query_row, key_row = query_gain[None], key_gain[None]

    merged = call(
        functools.partial(merge_kernel, head_dim, bounds),
        [((cells, 2 * width), BF16) for width in widths] * 2,
        [key_rows, value_rows, merge_cells[0].T, key_row],
        scratch=[((tok, lanes), BF16)] * 2
        + [(merge_cells.shape[:0:-1], jnp.int32), ((1, head_dim), F32)],
        far_in=4,
        copies=2 + 4 * sum(len(pieces(width)) for width in widths),
        vmem=ALL_VMEM_BYTES,
    )
    crossed = [exchange(sent, "seq", 1) for sent in merged[len(bounds) :]]
    crossed, late_queries, late_upstream, late_keys = lax.optimization_barrier(
        (crossed, queries, upstream, key_rows)
    )
    gathered = [
        chip_gather(jnp.concatenate([own, other], axis=0), chips)
        for own, other in zip(merged, crossed)
    ]

    (packed,) = call(
        pack_kernel, [((tok, lanes), BF16)], [late_queries, late_upstream], far_in=2, copies=2
    )
    query_unit, query_scale, normed, both_upstream = call(
        functools.partial(query_kernel, head_dim),
        [((CORES * tok, half), F32)] * 2 + [((CORES * tok, half), BF16)] * 2,
        [queries, upstream, exchange(packed, "seq", 1), query_row],
        copies=1,
    )
    key_unit, key_scale, table, gain_row = call(
        functools.partial(key_kernel, head_dim),
        [((tok, lanes), F32)] * 2 + [((tok, 2 * cells), BF16), ((1, 2 * TILE), F32)],
        [late_keys, unmerge, key_row],
    )

    group = min(chips, 4)
    results = [
        call(
            functools.partial(attend_kernel, head_dim, start, chips, group),
            [
                ((CORES * tok, width), BF16),
                ((CORES * tok, width), F32),
                ((1, 2 * head_dim), F32),
                ((CORES * cells, 2 * width), F32),
            ]
            + [((CORES * cells, 2 * width), BF16)] * (chips - 1),
            [normed, both_upstream] + blocks,
            micros=3.5 * width / half,
        )
        for (start, stop), width, blocks in zip(bounds, widths, gathered)
    ]
    attended = [result[0] for result in results]
    grads = [result[1] for result in results]
    rest = Rest(sum(result[2] for result in results), chips)

    first_steps, next_steps, last_steps = OPT["steps"].split("|")

    def query_back():
        return call(
            functools.partial(query_back_kernel, head_dim, bounds),
            [((tok, lanes), BF16)] * 3,
            [query_unit, query_scale, query_row] + attended + grads,
            scratch=[((tok, half), BF16)] * 2,
            far_out=2,
            copies=2,
            micros=OPT["kc"],
        )

    parts = [result[3:] for result in results]
    far = [chip_reduce(part[: chips // 2 - 1 : -1]) if chips > 1 else [] for part in parts]
    rest.advance(first_steps)
    if OPT["k4"] == 1:
        attended_half, grad_half, sent_part = query_back()
        if OPT["k4"] == 1:
            far, sent_part = lax.optimization_barrier((far, sent_part))
    if OPT["hb"]:
        far, rest.gains = lax.optimization_barrier((far, rest.gains))
    mirror = CORES * (chips - 1)
    sums = [added(terms).astype(BF16) for terms in far if terms]
    if OPT["sb"] == 1:
        sums, rest.gains = lax.optimization_barrier((sums, rest.gains))
    if OPT["sb"] == 2:
        _, rest.gains = lax.optimization_barrier((sums, rest.gains))
    if OPT["split"]:
        straight = [[exchange(sent[:cells], "seq", mirror)] for sent in sums]
        across = [[exchange(sent[cells:], "seq", mirror + 1)] for sent in sums]
    else:
        straight = [[exchange(sent, "seq", mirror)] for sent in sums]
        across = [[] for _ in bounds]
    if chips == 1:
        straight = across = [[] for _ in bounds]
    near = [chip_reduce(part[: max(chips // 2, 1)]) for part in parts]
    if OPT["split"]:
        crossed = [exchange(added([term[cells:] for term in terms]), "seq", 1) for terms in near]
    else:
        crossed = None
    if OPT["k4"] != 1:
        attended_half, grad_half, sent_part = query_back()
    if OPT["near"] == 1:
        rest.advance(next_steps[:1])
        near, rest.gains = lax.optimization_barrier((near, rest.gains))
        rest.advance(next_steps[1:])
    elif OPT["near"] == 2:
        near, rest.gains = lax.optimization_barrier((near, rest.gains))
        rest.advance(next_steps)
    else:
        rest.advance(next_steps)
    arrived_part = exchange(sent_part, "seq", 1)
    straight, across, crossed, rest.gains, arrived_part = lax.optimization_barrier(
        (straight, across, crossed, rest.gains, arrived_part)
    )
    own_terms = [first + last for first, last in zip(near, straight)]
    if not OPT["split"]:
        crossed = [exchange(added([t[cells:] for t in terms]), "seq", 1) for terms in own_terms]
    rest.advance(last_steps)
    gain_total = rest.gains[0]

    sources = []
    for chunk in range(len(bounds)):
        sources += own_terms[chunk] + [crossed[chunk]] + across[chunk]
    grad_key, grad_value, attended_all, grad_query = call(
        functools.partial(key_back_kernel, head_dim, bounds, len(own_terms[0]), 1 + len(across[0])),
        [((tok, lanes), BF16)] * 4,
        [attended_half, grad_half, arrived_part, key_unit, key_scale, table, gain_row] + sources,
        scratch=[((CORES, tok, half), BF16)] * 2,
        far_in=2,
        far_out=4,
        copies=2 * CORES + 2,
        aliases={0: 2, 1: 3},
        micros=2.0,
    )
    return (
        attended_all[None],
        grad_query[None],
        grad_key[None],
        grad_value[None],
        gain_total[:head_dim] / query_gain,
        gain_total[head_dim:] / key_gain,
    )


def solution(mesh):
    rows = P("img", "seq", None)
    return jax.shard_map(
        local,
        mesh=mesh,
        in_specs=(rows, rows, rows, rows, P("img", "seq"), rows, P(), P()),
        out_specs=(rows, rows, rows, rows, P(), P()),
        check_vma=False,
    )
```

```python
import functools
import math

import jax
import jax.numpy as jnp
from jax import lax
from jax.experimental import pallas as pl
from jax.experimental.pallas import tpu as pltpu
from jax.sharding import PartitionSpec as P

EPSILON = 1e-06
TILE = 128
CORES = 2
BF16 = jnp.bfloat16
F32 = jnp.float32
VMEM_BYTES = 40 * 1024 * 1024
ALL_VMEM_BYTES = 62 * 1024 * 1024


def call(kernel, out_shapes, inputs, scratch=(), far_in=0, far_out=0, copies=0, aliases=None, vmem=VMEM_BYTES, micros=1.0):
    near, far = pl.BlockSpec(memory_space=pltpu.VMEM), pl.BlockSpec(memory_space=pltpu.HBM)
    buffers = [pltpu.VMEM(shape, kind) for shape, kind in scratch]
    if copies:
        buffers.append(pltpu.SemaphoreType.DMA((copies,)))
    return pl.pallas_call(
        kernel,
        out_shape=[jax.ShapeDtypeStruct(shape, kind) for shape, kind in out_shapes],
        in_specs=[far] * far_in + [near] * (len(inputs) - far_in),
        out_specs=[far] * far_out + [near] * (len(out_shapes) - far_out),
        scratch_shapes=buffers,
        input_output_aliases=aliases or {},
        cost_estimate=pl.CostEstimate(
            flops=int(micros * 1e9), bytes_accessed=int(micros * 2e6), transcendentals=0
        ),
        compiler_params=pltpu.CompilerParams(vmem_limit_bytes=vmem),
    )(*inputs)


def core_side():
    return lax.rem(lax.axis_index("seq"), CORES)


def lanes_at(index, width=TILE):
    return pl.ds(pl.multiple_of(index * TILE, TILE), width)


def pieces(width):
    return [(at, min(at + 2 * TILE, width)) for at in range(0, width, 2 * TILE)]


def dot(left, right, contract=((1,), (0,))):
    return lax.dot_general(left, right, (contract, ((), ())), preferred_element_type=F32)


def halves(array):
    high = array.astype(BF16)
    return high, (array - high.astype(F32)).astype(BF16)


def over_heads(array, head_dim, finish):
    head = lax.broadcasted_iota(jnp.int32, (1, TILE), 1) // head_dim
    tiles = []
    for at in range(0, array.shape[1], TILE):
        tile = array[:, at : at + TILE]
        result = None
        for index in range(TILE // head_dim):
            total = jnp.sum(jnp.where(head == index, tile, 0.0), axis=1, keepdims=True)
            value = finish(total * (1.0 / head_dim))
            result = value if result is None else jnp.where(head == index, value, result)
        tiles.append(jnp.broadcast_to(result, tile.shape))
    return jnp.concatenate(tiles, axis=1)


def unit_rows(array, head_dim):
    scale = over_heads(array * array, head_dim, lambda mean: lax.rsqrt(mean + EPSILON))
    return array * scale, scale


def norm_back(grad_normed, unit_vals, scale, gain_row, head_dim):
    grad_unit = grad_normed * gain_row
    mean_inner = over_heads(grad_unit * unit_vals, head_dim, lambda mean: mean)
    return scale * (grad_unit - unit_vals * mean_inner)


def gain_lanes(gain_ref, width):
    row = gain_ref[...]
    return jnp.concatenate([row] * (width // row.shape[1]), axis=1)


def merge_kernel(head_dim, bounds, key_ref, value_ref, cells_ref, gain_ref, *refs):
    count = len(bounds)
    own_refs, send_refs = refs[:count], refs[count : 2 * count]
    key_buf, value_buf, cells_buf, gain_buf, copied = refs[2 * count :]
    tok, lanes = key_buf.shape
    half = lanes // CORES
    cells = cells_ref.shape[1]
    side = core_side()
    small = [
        pltpu.make_async_copy(cells_ref, cells_buf, copied.at[0]),
        pltpu.make_async_copy(gain_ref, gain_buf, copied.at[1]),
    ]
    for move in small:
        move.start()
    spans = [
        (other, chunk, start, stop, start + at, start + to)
        for other in (1, 0)
        for chunk, (start, stop) in enumerate(bounds)
        for at, to in pieces(stop - start)
    ]
    moves = []
    for index, (other, _, _, _, at, to) in enumerate(spans):
        source = lanes_at((1 - side if other else side) * (half // TILE) + at // TILE, to - at)
        here = slice(other * half + at, other * half + to)
        for which, (far, near) in enumerate(((key_ref, key_buf), (value_ref, value_buf))):
            move = pltpu.make_async_copy(
                far.at[:, source], near.at[:, here], copied.at[2 + 2 * index + which]
            )
            move.start()
            moves.append(move)
    for move in small:
        move.wait()
    listed = lax.rem(cells_buf[...], tok)
    ids = lax.broadcasted_iota(jnp.int32, (tok, cells), 0)
    member = sum((listed[j : j + 1] == ids).astype(F32) for j in range(cells_ref.shape[0]))
    member = member.T.astype(BF16)
    twice = jnp.concatenate([member, member], axis=1)
    for index, (other, chunk, start, stop, at, to) in enumerate(spans):
        here = slice(other * half + at, other * half + to)
        out_ref = (send_refs if other else own_refs)[chunk]
        if index % (len(spans) // CORES) == 0:
            for move in moves[2 * index : 2 * index + 2 * len(spans) // CORES]:
                move.wait()
        unit_vals, _ = unit_rows(key_buf[:, here].astype(F32), head_dim)
        keys = dot(twice, jnp.concatenate(halves(unit_vals), axis=0))
        keys *= gain_lanes(gain_buf, to - at) * 0.25
        out_ref[:, at - start : to - start] = keys.astype(BF16)
        values = dot(member, value_buf[:, here]) * 0.25
        out_ref[:, stop - 2 * start + at : stop - 2 * start + to] = values.astype(BF16)


def pack_kernel(query_ref, upstream_ref, send_ref, copied):
    half = query_ref.shape[1] // CORES
    source = lanes_at((1 - core_side()) * (half // TILE), half)
    moves = [
        pltpu.make_async_copy(query_ref.at[:, source], send_ref.at[:, :half], copied.at[0]),
        pltpu.make_async_copy(upstream_ref.at[:, source], send_ref.at[:, half:], copied.at[1]),
    ]
    for move in moves:
        move.start()
    for move in moves:
        move.wait()


def query_kernel(
    head_dim, query_ref, upstream_ref, arrived_ref, gain_ref, unit_ref, scale_ref, *refs
):
    out_ref, grad_ref, copied = refs
    tok, lanes = query_ref.shape
    half = lanes // CORES
    side = core_side()
    source = lanes_at(side * (half // TILE), half)
    move = pltpu.make_async_copy(upstream_ref.at[:, source], grad_ref.at[:tok], copied.at[0])
    move.start()
    grad_ref[tok:] = arrived_ref[:, half:]
    for at, to in pieces(half):
        for row, queries in (
            (0, query_ref[:, lanes_at(side * (half // TILE) + at // TILE, to - at)]),
            (tok, arrived_ref[:, at:to]),
        ):
            here = slice(row, row + tok)
            unit_vals, scale = unit_rows(queries.astype(F32), head_dim)
            unit_ref[here, at:to] = unit_vals
            scale_ref[here, at:to] = scale
            out_ref[here, at:to] = (unit_vals * gain_lanes(gain_ref, to - at)).astype(BF16)
    move.wait()


def key_kernel(head_dim, key_ref, unmerge_ref, gain_ref, unit_ref, scale_ref, table_ref, row_ref):
    tok = key_ref.shape[0]
    cells = table_ref.shape[1] // 2
    owner = lax.rem(unmerge_ref[...], cells)
    table = (lax.broadcasted_iota(jnp.int32, (cells, tok), 0) == owner).astype(F32) * 0.25
    table = table.T.astype(BF16)
    table_ref[...] = jnp.concatenate([table, table], axis=1)
    row_ref[...] = gain_lanes(gain_ref, row_ref.shape[1])
    for at, to in pieces(key_ref.shape[1]):
        unit_vals, scale = unit_rows(key_ref[:, at:to].astype(F32), head_dim)
        unit_ref[:, at:to] = unit_vals
        scale_ref[:, at:to] = scale


def attend_kernel(head_dim, start, blocks, group, *refs):
    query_ref, upstream_ref = refs[:2]
    block_refs = refs[2 : 2 + blocks]
    attended_ref, grad_ref, gain_out_ref = refs[2 + blocks : 5 + blocks]
    part_refs = refs[5 + blocks :]
    rows = query_ref.shape[0]
    block_rows, width = block_refs[0].shape
    width = width // 2
    per = TILE // head_dim
    cells = group * block_rows
    scale = head_dim**-0.5
    exponent = scale * math.log2(math.e)
    lane_head = lax.broadcasted_iota(jnp.int32, (1, TILE), 1) // head_dim
    cell_heads = lax.broadcasted_iota(jnp.int32, (cells, TILE), 1) // head_dim
    masks = [(cell_heads == head).astype(F32).astype(BF16) for head in range(per)]

    heads = range(per)

    def spread(array):
        return jnp.concatenate([array * mask for mask in masks], axis=0)

    def by_lane(parts):
        result = parts[0]
        for head in range(1, per):
            result = jnp.where(lane_head == head, parts[head], result)
        return result

    def per_head(left, rights, contract):
        return jnp.concatenate(
            [
                dot(left[h * head_dim : (h + 1) * head_dim], rights[h], ((1,), (contract,)))
                for h in heads
            ],
            axis=0,
        ).T

    def forward(tile):
        lane = lanes_at(tile)
        value_lane = lanes_at(width // TILE + tile)
        source = lanes_at(start // TILE + tile)
        queries = query_ref[:, source]
        upstream = upstream_ref[:, source]
        weighted = jnp.zeros((rows, TILE), F32)
        totals = [jnp.zeros((rows, 1), F32) for _ in heads]
        held = []
        for first in range(0, blocks, group):
            members = block_refs[first : first + group]
            keys = jnp.concatenate([ref[:, lane] for ref in members], axis=0)
            values = jnp.concatenate([ref[:, value_lane] for ref in members], axis=0)
            scores = dot(queries, spread(keys), ((1,), (1,)))
            exp_scores = jnp.exp2(scores * exponent)
            exp_parts = [exp_scores[:, h * cells : (h + 1) * cells] for h in heads]
            weighted += dot(exp_scores.astype(BF16), spread(values))
            totals = [
                total + jnp.sum(part, axis=1, keepdims=True)
                for total, part in zip(totals, exp_parts)
            ]
            held.append((keys, dot(upstream, spread(values), ((1,), (1,))), exp_parts))
        inverses = [1.0 / total for total in totals]
        attended = (weighted * by_lane(inverses)).astype(BF16)
        attended_ref[:, lane] = attended
        products = upstream.astype(F32) * attended.astype(F32)
        inners = [
            jnp.sum(jnp.where(lane_head == h, products, 0.0), axis=1, keepdims=True) for h in heads
        ]
        return queries, upstream, held, inverses, inners

    def backward(tile, kept, sums):
        query_sum, key_sum = sums
        queries, upstream, held, inverses, inners = kept
        lane = lanes_at(tile)
        value_lane = lanes_at(width // TILE + tile)
        queries_turned, upstream_turned = queries.T, upstream.T
        grad_queries = jnp.zeros((rows, TILE), F32)
        for index, (keys, grad_weights, exp_parts) in enumerate(held):
            attention = [part * inverse for part, inverse in zip(exp_parts, inverses)]
            grad_scores = [
                (attention[h] * (grad_weights[:, h * cells : (h + 1) * cells] - inners[h])).astype(
                    BF16
                )
                for h in heads
            ]
            grad_queries += dot(jnp.concatenate(grad_scores, axis=1), spread(keys))
            grad_keys = per_head(queries_turned, grad_scores, 0) * scale
            grad_values = per_head(upstream_turned, [part.astype(BF16) for part in attention], 0)
            key_sum += jnp.sum(grad_keys * keys.astype(F32), axis=0, keepdims=True)
            for member in range(group):
                ref = part_refs[index * group + member]
                here = slice(member * block_rows, (member + 1) * block_rows)
                ref[:, lane] = grad_keys[here].astype(ref.dtype)
                ref[:, value_lane] = grad_values[here].astype(ref.dtype)
        grad_queries *= scale
        grad_ref[:, lane] = grad_queries
        query_sum += jnp.sum(grad_queries * queries.astype(F32), axis=0, keepdims=True)
        return query_sum, key_sum

    sums = (jnp.zeros((1, TILE), F32), jnp.zeros((1, TILE), F32))
    if blocks == group:
        kept = forward(0)
        for tile in range(width // TILE):
            ahead = forward(tile + 1) if tile + 1 < width // TILE else None
            sums = backward(tile, kept, sums)
            kept = ahead
    else:
        sums = lax.fori_loop(
            0, width // TILE, lambda tile, sums: backward(tile, forward(tile), sums), sums
        )

    def per_channel(row):
        return sum(row[:, at : at + head_dim] for at in range(0, TILE, head_dim))

    gain_out_ref[...] = jnp.concatenate([per_channel(row) for row in sums], axis=1)


def query_back_kernel(head_dim, bounds, unit_ref, scale_ref, gain_ref, *refs):
    count = len(bounds)
    attended_refs, grad_refs = refs[:count], refs[count : 2 * count]
    attended_out, grad_out, send_ref, attended_buf, grad_buf, copied = refs[2 * count :]
    tok, half = attended_buf.shape
    for (start, stop), attended_ref, grad_ref in zip(bounds, attended_refs, grad_refs):
        attended_buf[:, start:stop] = attended_ref[:tok]
        send_ref[:, start:stop] = attended_ref[tok:]
        for at, to in pieces(stop - start):
            lane = slice(start + at, start + to)
            grads = norm_back(
                grad_ref[:, at:to],
                unit_ref[:, lane],
                scale_ref[:, lane],
                gain_lanes(gain_ref, to - at),
                head_dim,
            ).astype(BF16)
            grad_buf[:, lane] = grads[:tok]
            send_ref[:, half + start + at : half + start + to] = grads[tok:]
    place = lanes_at(core_side() * (half // TILE), half)
    moves = [
        pltpu.make_async_copy(attended_buf, attended_out.at[:, place], copied.at[0]),
        pltpu.make_async_copy(grad_buf, grad_out.at[:, place], copied.at[1]),
    ]
    for move in moves:
        move.start()
    for move in moves:
        move.wait()


def key_back_kernel(head_dim, bounds, own_terms, other_terms, *refs):
    query_refs, refs = refs[2:3], refs[3:]
    unit_ref, scale_ref, table_ref, gain_ref = refs[:4]
    refs = refs[4:]
    sources = []
    for _ in bounds:
        sources.append((refs[:own_terms], refs[own_terms : own_terms + other_terms]))
        refs = refs[own_terms + other_terms :]
    grad_key_out, grad_value_out, *query_outs, grad_key_buf, grad_value_buf, copied = refs
    tok, half = grad_key_buf.shape[1:]
    cells = sources[0][1][0].shape[0]
    side = core_side()
    table = table_ref[...]

    def spread(chunk, other, at, to):
        total = added([ref[:cells, at:to] for ref in sources[chunk][other]])
        return dot(table, jnp.concatenate(halves(total), axis=0))

    spans = [
        (other, chunk, start, stop, start + at, start + to)
        for other in range(CORES)
        for chunk, (start, stop) in enumerate(bounds)
        for at, to in pieces(stop - start)
    ]
    moves = []

    def send(buf, out, other):
        place = lanes_at((1 - side if other else side) * (half // TILE), half)
        move = pltpu.make_async_copy(buf, out.at[:, place], copied.at[len(moves)])
        move.start()
        moves.append(move)

    for index, out in enumerate(query_outs):
        send(query_refs[0].at[:, index * half : (index + 1) * half], out, 1)
    for other, chunk, start, stop, at, to in spans:
        grad_value_buf[other, :, at:to] = spread(
            chunk, other, stop - 2 * start + at, stop - 2 * start + to
        ).astype(BF16)
    for other in range(CORES):
        send(grad_value_buf.at[other], grad_value_out, other)
    for other, chunk, start, stop, at, to in spans:
        first = (1 - side if other else side) * (half // TILE)
        lane = lanes_at(first + at // TILE, to - at)
        grad_key_buf[other, :, at:to] = norm_back(
            spread(chunk, other, at - start, to - start),
            unit_ref[:, lane],
            scale_ref[:, lane],
            gain_ref[:, : to - at],
            head_dim,
        ).astype(BF16)
        if to == half:
            send(grad_key_buf.at[other], grad_key_out, other)
    for move in moves:
        move.wait()


def exchange(array, axis, apart):
    return lax.ppermute(array, axis, [(i, i ^ apart) for i in range(lax.axis_size(axis))])


def chip_gather(block, chips):
    if chips == 1:
        return [block]
    mirrored = exchange(block, "seq", CORES * (chips - 1))
    return chip_gather(block, chips // 2) + chip_gather(mirrored, chips // 2)[::-1]


def chip_reduce(parts):
    chips = len(parts)
    if chips == 1:
        return [parts[0]]
    sent = added(chip_reduce(parts[: chips // 2 - 1 : -1])).astype(BF16)
    return chip_reduce(parts[: chips // 2]) + [exchange(sent, "seq", CORES * (chips - 1))]


def added(terms):
    total = terms[0].astype(F32)
    for term in terms[1:]:
        total += term.astype(F32)
    return total


class Rest:
    def __init__(self, gains, chips):
        self.gains = gains
        images = lax.axis_size("img")
        image_steps = [("img", 1 << bit) for bit in range(images.bit_length() - 1)]
        chip_steps = [("seq", CORES << bit) for bit in range(chips.bit_length() - 1)]
        self.table = {
            "c": [("seq", 1)],
            "I": [("img", *range(1, images))],
            "y": image_steps[:1],
            "x": image_steps[1:],
            "z": chip_steps[:1],
            "w": chip_steps[1:],
            "D": [("seq", *(CORES * apart for apart in range(1, chips)))],
        }

    def advance(self, names):
        for name in names:
            for axis, *aparts in self.table[name]:
                arrived = [exchange(self.gains, axis, apart) for apart in aparts]
                self.gains = sum(arrived, self.gains)


OPT = dict(tc=1, split=0, steps="cD|yx|", near=1, hb=0, sb=2, k4=4, kc=0.1, pc=1.0)


def chunk_bounds(half):
    return ((0, half),)


def local(query_proj, key_proj, value_proj, merge_cells, unmerge, grad_out, query_gain, key_gain):
    queries, key_rows, value_rows = query_proj[0], key_proj[0], value_proj[0]
    upstream = grad_out[0]
    tok, lanes = queries.shape
    half = lanes // CORES
    head_dim = query_gain.shape[0]
    cells = merge_cells.shape[1]
    chips = lax.axis_size("seq") // CORES
    bounds = chunk_bounds(half)
    widths = [stop - start for start, stop in bounds]
    query_row, key_row = query_gain[None], key_gain[None]

    merged = call(
        functools.partial(merge_kernel, head_dim, bounds),
        [((cells, 2 * width), BF16) for width in widths] * 2,
        [key_rows, value_rows, merge_cells[0].T, key_row],
        scratch=[((tok, lanes), BF16)] * 2
        + [(merge_cells.shape[:0:-1], jnp.int32), ((1, head_dim), F32)],
        far_in=4,
        copies=2 + 4 * sum(len(pieces(width)) for width in widths),
        vmem=ALL_VMEM_BYTES,
    )
    crossed = [exchange(sent, "seq", 1) for sent in merged[len(bounds) :]]
    crossed, late_queries, late_upstream, late_keys = lax.optimization_barrier(
        (crossed, queries, upstream, key_rows)
    )
    gathered = [
        chip_gather(jnp.concatenate([own, other], axis=0), chips)
        for own, other in zip(merged, crossed)
    ]

    (packed,) = call(
        pack_kernel, [((tok, lanes), BF16)], [late_queries, late_upstream], far_in=2, copies=2
    )
    query_unit, query_scale, normed, both_upstream = call(
        functools.partial(query_kernel, head_dim),
        [((CORES * tok, half), F32)] * 2 + [((CORES * tok, half), BF16)] * 2,
        [queries, upstream, exchange(packed, "seq", 1), query_row],
        copies=1,
    )
    key_unit, key_scale, table, gain_row = call(
        functools.partial(key_kernel, head_dim),
        [((tok, lanes), F32)] * 2 + [((tok, 2 * cells), BF16), ((1, 2 * TILE), F32)],
        [late_keys, unmerge, key_row],
    )

    group = min(chips, 4)
    results = [
        call(
            functools.partial(attend_kernel, head_dim, start, chips, group),
            [
                ((CORES * tok, width), BF16),
                ((CORES * tok, width), F32),
                ((1, 2 * head_dim), F32),
                ((CORES * cells, 2 * width), F32),
            ]
            + [((CORES * cells, 2 * width), BF16)] * (chips - 1),
            [normed, both_upstream] + blocks,
            micros=3.5 * width / half,
        )
        for (start, stop), width, blocks in zip(bounds, widths, gathered)
    ]
    attended = [result[0] for result in results]
    grads = [result[1] for result in results]
    rest = Rest(sum(result[2] for result in results), chips)

    first_steps, next_steps, last_steps = OPT["steps"].split("|")

    def query_back():
        return call(
            functools.partial(query_back_kernel, head_dim, bounds),
            [((tok, lanes), BF16)] * 3,
            [query_unit, query_scale, query_row] + attended + grads,
            scratch=[((tok, half), BF16)] * 2,
            far_out=2,
            copies=2,
            micros=OPT["kc"],
        )

    parts = [result[3:] for result in results]
    far = [chip_reduce(part[: chips // 2 - 1 : -1]) if chips > 1 else [] for part in parts]
    rest.advance(first_steps)
    if OPT["k4"] == 1:
        attended_half, grad_half, sent_part = query_back()
        if OPT["k4"] == 1:
            far, sent_part = lax.optimization_barrier((far, sent_part))
    if OPT["hb"]:
        far, rest.gains = lax.optimization_barrier((far, rest.gains))
    mirror = CORES * (chips - 1)
    sums = [added(terms).astype(BF16) for terms in far if terms]
    if OPT["sb"] == 1:
        sums, rest.gains = lax.optimization_barrier((sums, rest.gains))
    if OPT["sb"] == 2:
        _, rest.gains = lax.optimization_barrier((sums, rest.gains))
    if OPT["split"]:
        straight = [[exchange(sent[:cells], "seq", mirror)] for sent in sums]
        across = [[exchange(sent[cells:], "seq", mirror + 1)] for sent in sums]
    else:
        straight = [[exchange(sent, "seq", mirror)] for sent in sums]
        across = [[] for _ in bounds]
    if chips == 1:
        straight = across = [[] for _ in bounds]
    near = [chip_reduce(part[: max(chips // 2, 1)]) for part in parts]
    if OPT["tc"]:
        near_crossed = [exchange(added([t[cells:] for t in terms]), "seq", 1) for terms in near]
    if OPT["split"]:
        crossed = [exchange(added([term[cells:] for term in terms]), "seq", 1) for terms in near]
    else:
        crossed = None
    if OPT["k4"] == 4:
        _, query_unit = lax.optimization_barrier((near, query_unit))
    if OPT["k4"] == 5:
        _, query_unit = lax.optimization_barrier((sums, query_unit))
    if OPT["k4"] in (0, 2, 4, 5):
        attended_half, grad_half, sent_part = query_back()
    if OPT["near"] == 1:
        rest.advance(next_steps[:1])
        near, rest.gains = lax.optimization_barrier((near, rest.gains))
        if OPT["k4"] == 3:
            query_unit, rest.gains = lax.optimization_barrier((query_unit, rest.gains))
            attended_half, grad_half, sent_part = query_back()
        rest.advance(next_steps[1:])
    elif OPT["near"] == 2:
        near, rest.gains = lax.optimization_barrier((near, rest.gains))
        rest.advance(next_steps)
    else:
        rest.advance(next_steps)
    arrived_part = exchange(sent_part, "seq", 1)
    if OPT["tc"]:
        straight, near_crossed, rest.gains, arrived_part = lax.optimization_barrier(
            (straight, near_crossed, rest.gains, arrived_part)
        )
    else:
        straight, rest.gains, arrived_part = lax.optimization_barrier(
            (straight, rest.gains, arrived_part)
        )
    own_terms = [first + last for first, last in zip(near, straight)]
    if OPT["tc"] and chips > 1:
        crossed = near_crossed
        across = [[exchange(term[cells:], "seq", 1) for term in terms] for terms in straight]
    elif not OPT["split"]:
        crossed = [exchange(added([t[cells:] for t in terms]), "seq", 1) for terms in own_terms]
    rest.advance(last_steps)
    gain_total = rest.gains[0]

    sources = []
    for chunk in range(len(bounds)):
        sources += own_terms[chunk] + [crossed[chunk]] + across[chunk]
    grad_key, grad_value, attended_all, grad_query = call(
        functools.partial(key_back_kernel, head_dim, bounds, len(own_terms[0]), 1 + len(across[0])),
        [((tok, lanes), BF16)] * 4,
        [attended_half, grad_half, arrived_part, key_unit, key_scale, table, gain_row] + sources,
        scratch=[((CORES, tok, half), BF16)] * 2,
        far_in=2,
        far_out=4,
        copies=2 * CORES + 2,
        aliases={0: 2, 1: 3},
        micros=2.0,
    )
    return (
        attended_all[None],
        grad_query[None],
        grad_key[None],
        grad_value[None],
        gain_total[:head_dim] / query_gain,
        gain_total[head_dim:] / key_gain,
    )


def solution(mesh):
    rows = P("img", "seq", None)
    return jax.shard_map(
        local,
        mesh=mesh,
        in_specs=(rows, rows, rows, rows, P("img", "seq"), rows, P(), P()),
        out_specs=(rows, rows, rows, rows, P(), P()),
        check_vma=False,
    )
```

```python
import functools
import math

import jax
import jax.numpy as jnp
from jax import lax
from jax.experimental import pallas as pl
from jax.experimental.pallas import tpu as pltpu
from jax.sharding import PartitionSpec as P

EPSILON = 1e-06
TILE = 128
CORES = 2
BF16 = jnp.bfloat16
F32 = jnp.float32
VMEM_BYTES = 40 * 1024 * 1024
ALL_VMEM_BYTES = 62 * 1024 * 1024
OWN_VMEM_BYTES = 40 * 1024 * 1024


def call(kernel, out_shapes, inputs, scratch=(), far_in=0, far_out=0, copies=0, aliases=None, vmem=VMEM_BYTES, micros=1.0):
    near, far = pl.BlockSpec(memory_space=pltpu.VMEM), pl.BlockSpec(memory_space=pltpu.HBM)
    buffers = [pltpu.VMEM(shape, kind) for shape, kind in scratch]
    if copies:
        buffers.append(pltpu.SemaphoreType.DMA((copies,)))
    return pl.pallas_call(
        kernel,
        out_shape=[jax.ShapeDtypeStruct(shape, kind) for shape, kind in out_shapes],
        in_specs=[far] * far_in + [near] * (len(inputs) - far_in),
        out_specs=[far] * far_out + [near] * (len(out_shapes) - far_out),
        scratch_shapes=buffers,
        input_output_aliases=aliases or {},
        cost_estimate=pl.CostEstimate(
            flops=int(micros * 1e9), bytes_accessed=int(micros * 2e6), transcendentals=0
        ),
        compiler_params=pltpu.CompilerParams(vmem_limit_bytes=vmem),
    )(*inputs)


def core_side():
    return lax.rem(lax.axis_index("seq"), CORES)


def lanes_at(index, width=TILE):
    return pl.ds(pl.multiple_of(index * TILE, TILE), width)


def pieces(width):
    return [(at, min(at + 2 * TILE, width)) for at in range(0, width, 2 * TILE)]


def dot(left, right, contract=((1,), (0,))):
    return lax.dot_general(left, right, (contract, ((), ())), preferred_element_type=F32)


def halves(array):
    high = array.astype(BF16)
    return high, (array - high.astype(F32)).astype(BF16)


def over_heads(array, head_dim, finish):
    head = lax.broadcasted_iota(jnp.int32, (1, TILE), 1) // head_dim
    tiles = []
    for at in range(0, array.shape[1], TILE):
        tile = array[:, at : at + TILE]
        result = None
        for index in range(TILE // head_dim):
            total = jnp.sum(jnp.where(head == index, tile, 0.0), axis=1, keepdims=True)
            value = finish(total * (1.0 / head_dim))
            result = value if result is None else jnp.where(head == index, value, result)
        tiles.append(jnp.broadcast_to(result, tile.shape))
    return jnp.concatenate(tiles, axis=1)


def unit_rows(array, head_dim):
    scale = over_heads(array * array, head_dim, lambda mean: lax.rsqrt(mean + EPSILON))
    return array * scale, scale


def norm_back(grad_normed, unit_vals, scale, gain_row, head_dim):
    grad_unit = grad_normed * gain_row
    mean_inner = over_heads(grad_unit * unit_vals, head_dim, lambda mean: mean)
    return scale * (grad_unit - unit_vals * mean_inner)


def gain_lanes(gain_ref, width):
    row = gain_ref[...]
    return jnp.concatenate([row] * (width // row.shape[1]), axis=1)


def merge_kernel(head_dim, bounds, other, key_ref, value_ref, cells_ref, gain_ref, *refs):
    count = len(bounds)
    out_refs = refs[:count]
    key_buf, value_buf, cells_buf, gain_buf, copied = refs[count:]
    tok, half = key_buf.shape
    cells = cells_ref.shape[1]
    side = core_side()
    small = [
        pltpu.make_async_copy(cells_ref, cells_buf, copied.at[0]),
        pltpu.make_async_copy(gain_ref, gain_buf, copied.at[1]),
    ]
    for move in small:
        move.start()
    spans = [
        (chunk, start, stop, start + at, start + to)
        for chunk, (start, stop) in enumerate(bounds)
        for at, to in pieces(stop - start)
    ]
    moves = []
    for index, (_, _, _, at, to) in enumerate(spans):
        source = lanes_at((1 - side if other else side) * (half // TILE) + at // TILE, to - at)
        here = slice(at, to)
        for which, (far, near) in enumerate(((key_ref, key_buf), (value_ref, value_buf))):
            move = pltpu.make_async_copy(
                far.at[:, source], near.at[:, here], copied.at[2 + 2 * index + which]
            )
            move.start()
            moves.append(move)
    for move in small + moves:
        move.wait()
    listed = lax.rem(cells_buf[...], tok)
    ids = lax.broadcasted_iota(jnp.int32, (tok, cells), 0)
    member = sum((listed[j : j + 1] == ids).astype(F32) for j in range(cells_ref.shape[0]))
    member = member.T.astype(BF16)
    twice = jnp.concatenate([member, member], axis=1)
    for chunk, start, stop, at, to in spans:
        here = slice(at, to)
        out_ref = out_refs[chunk]
        unit_vals, _ = unit_rows(key_buf[:, here].astype(F32), head_dim)
        keys = dot(twice, jnp.concatenate(halves(unit_vals), axis=0))
        keys *= gain_lanes(gain_buf, to - at) * 0.25
        out_ref[:, at - start : to - start] = keys.astype(BF16)
        values = dot(member, value_buf[:, here]) * 0.25
        out_ref[:, stop - 2 * start + at : stop - 2 * start + to] = values.astype(BF16)


def pack_kernel(query_ref, upstream_ref, send_ref, copied):
    half = query_ref.shape[1] // CORES
    source = lanes_at((1 - core_side()) * (half // TILE), half)
    moves = [
        pltpu.make_async_copy(query_ref.at[:, source], send_ref.at[:, :half], copied.at[0]),
        pltpu.make_async_copy(upstream_ref.at[:, source], send_ref.at[:, half:], copied.at[1]),
    ]
    for move in moves:
        move.start()
    for move in moves:
        move.wait()


def query_kernel(
    head_dim, query_ref, upstream_ref, arrived_ref, gain_ref, unit_ref, scale_ref, *refs
):
    out_ref, grad_ref, copied = refs
    tok, lanes = query_ref.shape
    half = lanes // CORES
    side = core_side()
    source = lanes_at(side * (half // TILE), half)
    move = pltpu.make_async_copy(upstream_ref.at[:, source], grad_ref.at[:tok], copied.at[0])
    move.start()
    grad_ref[tok:] = arrived_ref[:, half:]
    for at, to in pieces(half):
        for row, queries in (
            (0, query_ref[:, lanes_at(side * (half // TILE) + at // TILE, to - at)]),
            (tok, arrived_ref[:, at:to]),
        ):
            here = slice(row, row + tok)
            unit_vals, scale = unit_rows(queries.astype(F32), head_dim)
            unit_ref[here, at:to] = unit_vals
            scale_ref[here, at:to] = scale
            out_ref[here, at:to] = (unit_vals * gain_lanes(gain_ref, to - at)).astype(BF16)
    move.wait()


def key_kernel(head_dim, key_ref, unmerge_ref, gain_ref, unit_ref, scale_ref, table_ref, row_ref):
    tok = key_ref.shape[0]
    cells = table_ref.shape[1] // 2
    owner = lax.rem(unmerge_ref[...], cells)
    table = (lax.broadcasted_iota(jnp.int32, (cells, tok), 0) == owner).astype(F32) * 0.25
    table = table.T.astype(BF16)
    table_ref[...] = jnp.concatenate([table, table], axis=1)
    row_ref[...] = gain_lanes(gain_ref, row_ref.shape[1])
    for at, to in pieces(key_ref.shape[1]):
        unit_vals, scale = unit_rows(key_ref[:, at:to].astype(F32), head_dim)
        unit_ref[:, at:to] = unit_vals
        scale_ref[:, at:to] = scale


def attend_kernel(head_dim, start, blocks, group, *refs):
    query_ref, upstream_ref, unit_ref, scale_ref, gain_ref = refs[:5]
    block_refs = refs[5 : 5 + blocks]
    own_ref, send_ref, gain_out_ref = refs[5 + blocks : 8 + blocks]
    part_refs = refs[8 + blocks :]
    rows = query_ref.shape[0]
    block_rows, width = block_refs[0].shape
    width = width // 2
    per = TILE // head_dim
    cells = group * block_rows
    scale = head_dim**-0.5
    exponent = scale * math.log2(math.e)
    lane_head = lax.broadcasted_iota(jnp.int32, (1, TILE), 1) // head_dim
    cell_heads = lax.broadcasted_iota(jnp.int32, (cells, TILE), 1) // head_dim
    masks = [(cell_heads == head).astype(F32).astype(BF16) for head in range(per)]

    heads = range(per)

    def spread(array):
        return jnp.concatenate([array * mask for mask in masks], axis=0)

    def by_lane(parts):
        result = parts[0]
        for head in range(1, per):
            result = jnp.where(lane_head == head, parts[head], result)
        return result

    def per_head(left, rights, contract):
        return jnp.concatenate(
            [
                dot(left[h * head_dim : (h + 1) * head_dim], rights[h], ((1,), (contract,)))
                for h in heads
            ],
            axis=0,
        ).T

    def forward(tile):
        lane = lanes_at(tile)
        value_lane = lanes_at(width // TILE + tile)
        source = lanes_at(start // TILE + tile)
        queries = query_ref[:, source]
        upstream = upstream_ref[:, source]
        weighted = jnp.zeros((rows, TILE), F32)
        totals = [jnp.zeros((rows, 1), F32) for _ in heads]
        held = []
        for first in range(0, blocks, group):
            members = block_refs[first : first + group]
            keys = jnp.concatenate([ref[:, lane] for ref in members], axis=0)
            values = jnp.concatenate([ref[:, value_lane] for ref in members], axis=0)
            scores = dot(queries, spread(keys), ((1,), (1,)))
            exp_scores = jnp.exp2(scores * exponent)
            exp_parts = [exp_scores[:, h * cells : (h + 1) * cells] for h in heads]
            weighted += dot(exp_scores.astype(BF16), spread(values))
            totals = [
                total + jnp.sum(part, axis=1, keepdims=True)
                for total, part in zip(totals, exp_parts)
            ]
            held.append((keys, dot(upstream, spread(values), ((1,), (1,))), exp_parts))
        inverses = [1.0 / total for total in totals]
        attended = (weighted * by_lane(inverses)).astype(BF16)
        own_ref[:, lane] = attended[: rows // CORES]
        send_ref[:, lane] = attended[rows // CORES :]
        products = upstream.astype(F32) * attended.astype(F32)
        inners = [
            jnp.sum(jnp.where(lane_head == h, products, 0.0), axis=1, keepdims=True) for h in heads
        ]
        return queries, upstream, held, inverses, inners

    def backward(tile, kept, sums):
        query_sum, key_sum = sums
        queries, upstream, held, inverses, inners = kept
        lane = lanes_at(tile)
        value_lane = lanes_at(width // TILE + tile)
        queries_turned, upstream_turned = queries.T, upstream.T
        grad_queries = jnp.zeros((rows, TILE), F32)
        for index, (keys, grad_weights, exp_parts) in enumerate(held):
            attention = [part * inverse for part, inverse in zip(exp_parts, inverses)]
            grad_scores = [
                (attention[h] * (grad_weights[:, h * cells : (h + 1) * cells] - inners[h])).astype(
                    BF16
                )
                for h in heads
            ]
            grad_queries += dot(jnp.concatenate(grad_scores, axis=1), spread(keys))
            grad_keys = per_head(queries_turned, grad_scores, 0) * scale
            grad_values = per_head(upstream_turned, [part.astype(BF16) for part in attention], 0)
            key_sum += jnp.sum(grad_keys * keys.astype(F32), axis=0, keepdims=True)
            for member in range(group):
                ref = part_refs[index * group + member]
                here = slice(member * block_rows, (member + 1) * block_rows)
                ref[:, lane] = grad_keys[here].astype(ref.dtype)
                ref[:, value_lane] = grad_values[here].astype(ref.dtype)
        grad_queries *= scale
        grads = norm_back(
            grad_queries,
            unit_ref[:, lanes_at(start // TILE + tile)],
            scale_ref[:, lanes_at(start // TILE + tile)],
            gain_lanes(gain_ref, TILE),
            head_dim,
        ).astype(BF16)
        own_ref[:, value_lane] = grads[: rows // CORES]
        send_ref[:, value_lane] = grads[rows // CORES :]
        query_sum += jnp.sum(grad_queries * queries.astype(F32), axis=0, keepdims=True)
        return query_sum, key_sum

    sums = (jnp.zeros((1, TILE), F32), jnp.zeros((1, TILE), F32))
    if blocks == group:
        kept = forward(0)
        for tile in range(width // TILE):
            ahead = forward(tile + 1) if tile + 1 < width // TILE else None
            sums = backward(tile, kept, sums)
            kept = ahead
    else:
        sums = lax.fori_loop(
            0, width // TILE, lambda tile, sums: backward(tile, forward(tile), sums), sums
        )

    def per_channel(row):
        return sum(row[:, at : at + head_dim] for at in range(0, TILE, head_dim))

    gain_out_ref[...] = jnp.concatenate([per_channel(row) for row in sums], axis=1)


def place_kernel(bounds, *refs):
    count = len(bounds)
    own_refs, outs, copied = refs[:count], refs[count : count + 2], refs[count + 2]
    half = bounds[-1][1]
    moves = []
    for (start, stop), own_ref in zip(bounds, own_refs):
        width = stop - start
        place = lanes_at(core_side() * (half // TILE) + start // TILE, width)
        for index, out in enumerate(outs):
            source = own_ref.at[:, index * width : (index + 1) * width]
            moves.append(pltpu.make_async_copy(source, out.at[:, place], copied.at[len(moves)]))
            moves[-1].start()
    for move in moves:
        move.wait()


def key_back_kernel(head_dim, bounds, own_terms, other_terms, *refs):
    query_refs, refs = refs[2 : 2 + len(bounds)], refs[2 + len(bounds) :]
    unit_ref, scale_ref, table_ref, gain_ref = refs[:4]
    refs = refs[4:]
    sources = []
    for _ in bounds:
        sources.append((refs[:own_terms], refs[own_terms : own_terms + other_terms]))
        refs = refs[own_terms + other_terms :]
    grad_key_out, grad_value_out, *query_outs, grad_key_buf, grad_value_buf, copied = refs
    tok, half = grad_key_buf.shape[1:]
    cells = sources[0][1][0].shape[0]
    side = core_side()
    table = table_ref[...]

    def spread(chunk, other, at, to):
        total = added([ref[:cells, at:to] for ref in sources[chunk][other]])
        return dot(table, jnp.concatenate(halves(total), axis=0))

    spans = [
        (other, chunk, start, stop, start + at, start + to)
        for other in range(CORES)
        for chunk, (start, stop) in enumerate(bounds)
        for at, to in pieces(stop - start)
    ]
    moves = []

    def send(buf, out, other, start=0, width=half):
        first = (1 - side if other else side) * (half // TILE)
        place = lanes_at(first + start // TILE, width)
        move = pltpu.make_async_copy(buf, out.at[:, place], copied.at[len(moves)])
        move.start()
        moves.append(move)

    for (start, stop), ref in zip(bounds, query_refs):
        width = stop - start
        for index, out in enumerate(query_outs):
            send(ref.at[:, index * width : (index + 1) * width], out, 1, start, width)
    for other, chunk, start, stop, at, to in spans:
        grad_value_buf[other, :, at:to] = spread(
            chunk, other, stop - 2 * start + at, stop - 2 * start + to
        ).astype(BF16)
    for other in range(CORES):
        send(grad_value_buf.at[other], grad_value_out, other)
    for other, chunk, start, stop, at, to in spans:
        first = (1 - side if other else side) * (half // TILE)
        lane = lanes_at(first + at // TILE, to - at)
        grad_key_buf[other, :, at:to] = norm_back(
            spread(chunk, other, at - start, to - start),
            unit_ref[:, lane],
            scale_ref[:, lane],
            gain_ref[:, : to - at],
            head_dim,
        ).astype(BF16)
        if to == half:
            send(grad_key_buf.at[other], grad_key_out, other)
    for move in moves:
        move.wait()


def exchange(array, axis, apart):
    return lax.ppermute(array, axis, [(i, i ^ apart) for i in range(lax.axis_size(axis))])


def chip_gather(block, chips):
    if chips == 1:
        return [block]
    mirrored = exchange(block, "seq", CORES * (chips - 1))
    return chip_gather(block, chips // 2) + chip_gather(mirrored, chips // 2)[::-1]


def chip_reduce(parts):
    chips = len(parts)
    if chips == 1:
        return [parts[0]]
    sent = added(chip_reduce(parts[: chips // 2 - 1 : -1])).astype(BF16)
    return chip_reduce(parts[: chips // 2]) + [exchange(sent, "seq", CORES * (chips - 1))]


def added(terms):
    total = terms[0].astype(F32)
    for term in terms[1:]:
        total += term.astype(F32)
    return total


class Rest:
    def __init__(self, gains, chips):
        self.gains = gains
        images = lax.axis_size("img")
        image_steps = [("img", 1 << bit) for bit in range(images.bit_length() - 1)]
        chip_steps = [("seq", CORES << bit) for bit in range(chips.bit_length() - 1)]
        self.table = {
            "c": [("seq", 1)],
            "I": [("img", *range(1, images))],
            "y": image_steps[:1],
            "x": image_steps[1:],
            "z": chip_steps[:1],
            "w": chip_steps[1:],
            "D": [("seq", *(CORES * apart for apart in range(1, chips)))],
        }

    def advance(self, names):
        for name in names:
            for axis, *aparts in self.table[name]:
                arrived = [exchange(self.gains, axis, apart) for apart in aparts]
                self.gains = sum(arrived, self.gains)


OPT = dict(tl=2, km=2.0, tp=0, tc=1, split=0, steps="cD|yx|", near=1, hb=0, sb=2, pc=0.1)


def chunk_bounds(half):
    return ((0, half),)


def local(query_proj, key_proj, value_proj, merge_cells, unmerge, grad_out, query_gain, key_gain):
    queries, key_rows, value_rows = query_proj[0], key_proj[0], value_proj[0]
    upstream = grad_out[0]
    tok, lanes = queries.shape
    half = lanes // CORES
    head_dim = query_gain.shape[0]
    cells = merge_cells.shape[1]
    chips = lax.axis_size("seq") // CORES
    bounds = chunk_bounds(half)
    widths = [stop - start for start, stop in bounds]
    query_row, key_row = query_gain[None], key_gain[None]

    def merged_half(other):
        return call(
            functools.partial(merge_kernel, head_dim, bounds, other),
            [((cells, 2 * width), BF16) for width in widths],
            [key_rows, value_rows, merge_cells[0].T, key_row],
            scratch=[((tok, half), BF16)] * 2
            + [(merge_cells.shape[:0:-1], jnp.int32), ((1, head_dim), F32)],
            far_in=4,
            copies=2 + 2 * sum(len(pieces(width)) for width in widths),
            vmem=ALL_VMEM_BYTES if other else OWN_VMEM_BYTES,
            micros=0.5,
        )

    sent_half = merged_half(True)
    merged = merged_half(False)
    crossed = [exchange(sent, "seq", 1) for sent in sent_half]
    crossed, late_queries, late_upstream, late_keys = lax.optimization_barrier(
        (crossed, queries, upstream, key_rows)
    )
    gathered = [
        chip_gather(jnp.concatenate([own, other], axis=0), chips)
        for own, other in zip(merged, crossed)
    ]

    (packed,) = call(
        pack_kernel, [((tok, lanes), BF16)], [late_queries, late_upstream], far_in=2, copies=2
    )
    query_unit, query_scale, normed, both_upstream = call(
        functools.partial(query_kernel, head_dim),
        [((CORES * tok, half), F32)] * 2 + [((CORES * tok, half), BF16)] * 2,
        [queries, upstream, exchange(packed, "seq", 1), query_row],
        copies=1,
    )
    key_unit, key_scale, table, gain_row = call(
        functools.partial(key_kernel, head_dim),
        [((tok, lanes), F32)] * 2 + [((tok, 2 * cells), BF16), ((1, 2 * TILE), F32)],
        [late_keys, unmerge, key_row],
    )

    group = min(chips, 4)
    results = [
        call(
            functools.partial(attend_kernel, head_dim, start, chips, group),
            [
                ((tok, 2 * width), BF16),
                ((tok, 2 * width), BF16),
                ((1, 2 * head_dim), F32),
                ((CORES * cells, 2 * width), F32),
            ]
            + [((CORES * cells, 2 * width), BF16)] * (chips - 1),
            [normed, both_upstream, query_unit, query_scale, query_row] + blocks,
            micros=3.5 * width / half,
        )
        for (start, stop), width, blocks in zip(bounds, widths, gathered)
    ]
    rest = Rest(sum(result[2] for result in results), chips)

    first_steps, next_steps, last_steps = OPT["steps"].split("|")

    parts = [result[3:] for result in results]
    far = [chip_reduce(part[: chips // 2 - 1 : -1]) if chips > 1 else [] for part in parts]
    rest.advance(first_steps[:1])
    near_parts = [part[: max(chips // 2, 1)] for part in parts]
    if OPT["tp"]:
        _, near_parts = lax.optimization_barrier((rest.gains, near_parts))
    rest.advance(first_steps[1:])
    if OPT["hb"]:
        far, rest.gains = lax.optimization_barrier((far, rest.gains))
    mirror = CORES * (chips - 1)
    sums = [added(terms).astype(BF16) for terms in far if terms]
    if OPT["sb"] == 1:
        sums, rest.gains = lax.optimization_barrier((sums, rest.gains))
    if OPT["sb"] == 2:
        _, rest.gains = lax.optimization_barrier((sums, rest.gains))
    if OPT["split"]:
        straight = [[exchange(sent[:cells], "seq", mirror)] for sent in sums]
        across = [[exchange(sent[cells:], "seq", mirror + 1)] for sent in sums]
    else:
        straight = [[exchange(sent, "seq", mirror)] for sent in sums]
        across = [[] for _ in bounds]
    if chips == 1:
        straight = across = [[] for _ in bounds]
    near = [chip_reduce(part) for part in near_parts]
    if OPT["tc"]:
        near_crossed = [exchange(added([t[cells:] for t in terms]), "seq", 1) for terms in near]
    if OPT["split"]:
        crossed = [exchange(added([term[cells:] for term in terms]), "seq", 1) for terms in near]
    else:
        crossed = None
    if OPT["near"] == 1:
        rest.advance(next_steps[:1])
        near, rest.gains = lax.optimization_barrier((near, rest.gains))
        rest.advance(next_steps[1:])
    elif OPT["near"] == 2:
        near, rest.gains = lax.optimization_barrier((near, rest.gains))
        rest.advance(next_steps)
    else:
        rest.advance(next_steps)
    arrived_part = [exchange(result[1], "seq", 1) for result in results]
    attended_half, grad_half = call(
        functools.partial(place_kernel, bounds),
        [((tok, lanes), BF16)] * 2,
        [result[0] for result in results],
        far_out=2,
        copies=2 * len(bounds),
        micros=OPT["pc"],
    )
    if OPT["tl"] == 1:
        straight, rest.gains = lax.optimization_barrier((straight, rest.gains))
    elif OPT["tl"] == 2:
        pass
    elif OPT["tc"]:
        straight, near_crossed, rest.gains, arrived_part = lax.optimization_barrier(
            (straight, near_crossed, rest.gains, arrived_part)
        )
    else:
        straight, rest.gains, arrived_part = lax.optimization_barrier(
            (straight, rest.gains, arrived_part)
        )
    own_terms = [first + last for first, last in zip(near, straight)]
    if OPT["tc"] and chips > 1:
        crossed = near_crossed
        across = [[exchange(term[cells:], "seq", 1) for term in terms] for terms in straight]
    elif not OPT["split"]:
        crossed = [exchange(added([t[cells:] for t in terms]), "seq", 1) for terms in own_terms]
    if OPT["tl"] == 2:
        across, rest.gains = lax.optimization_barrier((across, rest.gains))
    rest.advance(last_steps)
    gain_total = rest.gains[0]

    sources = []
    for chunk in range(len(bounds)):
        sources += own_terms[chunk] + [crossed[chunk]] + across[chunk]
    grad_key, grad_value, attended_all, grad_query = call(
        functools.partial(key_back_kernel, head_dim, bounds, len(own_terms[0]), 1 + len(across[0])),
        [((tok, lanes), BF16)] * 4,
        [attended_half, grad_half]
        + arrived_part
        + [key_unit, key_scale, table, gain_row]
        + sources,
        scratch=[((CORES, tok, half), BF16)] * 2,
        far_in=2,
        far_out=4,
        copies=2 * CORES + 2 * len(bounds),
        aliases={0: 2, 1: 3},
        micros=OPT["km"],
    )
    return (
        attended_all[None],
        grad_query[None],
        grad_key[None],
        grad_value[None],
        gain_total[:head_dim] / query_gain,
        gain_total[head_dim:] / key_gain,
    )


def solution(mesh):
    rows = P("img", "seq", None)
    return jax.shard_map(
        local,
        mesh=mesh,
        in_specs=(rows, rows, rows, rows, P("img", "seq"), rows, P(), P()),
        out_specs=(rows, rows, rows, rows, P(), P()),
        check_vma=False,
    )
```

```python
import functools
import math

import jax
import jax.numpy as jnp
from jax import lax
from jax.experimental import pallas as pl
from jax.experimental.pallas import tpu as pltpu
from jax.sharding import PartitionSpec as P

EPSILON = 1e-06
TILE = 128
CORES = 2
BF16 = jnp.bfloat16
F32 = jnp.float32
VMEM_BYTES = 40 * 1024 * 1024
ALL_VMEM_BYTES = 62 * 1024 * 1024
OWN_VMEM_BYTES = 40 * 1024 * 1024


def call(kernel, out_shapes, inputs, scratch=(), far_in=0, far_out=0, copies=0, aliases=None, vmem=VMEM_BYTES, micros=1.0):
    near, far = pl.BlockSpec(memory_space=pltpu.VMEM), pl.BlockSpec(memory_space=pltpu.HBM)
    buffers = [pltpu.VMEM(shape, kind) for shape, kind in scratch]
    if copies:
        buffers.append(pltpu.SemaphoreType.DMA((copies,)))
    return pl.pallas_call(
        kernel,
        out_shape=[jax.ShapeDtypeStruct(shape, kind) for shape, kind in out_shapes],
        in_specs=[far] * far_in + [near] * (len(inputs) - far_in),
        out_specs=[far] * far_out + [near] * (len(out_shapes) - far_out),
        scratch_shapes=buffers,
        input_output_aliases=aliases or {},
        cost_estimate=pl.CostEstimate(
            flops=int(micros * 1e9), bytes_accessed=int(micros * 2e6), transcendentals=0
        ),
        compiler_params=pltpu.CompilerParams(vmem_limit_bytes=vmem),
    )(*inputs)


def core_side():
    return lax.rem(lax.axis_index("seq"), CORES)


def lanes_at(index, width=TILE):
    return pl.ds(pl.multiple_of(index * TILE, TILE), width)


def pieces(width):
    return [(at, min(at + 2 * TILE, width)) for at in range(0, width, 2 * TILE)]


def dot(left, right, contract=((1,), (0,))):
    return lax.dot_general(left, right, (contract, ((), ())), preferred_element_type=F32)


def halves(array):
    high = array.astype(BF16)
    return high, (array - high.astype(F32)).astype(BF16)


def over_heads(array, head_dim, finish):
    head = lax.broadcasted_iota(jnp.int32, (1, TILE), 1) // head_dim
    tiles = []
    for at in range(0, array.shape[1], TILE):
        tile = array[:, at : at + TILE]
        result = None
        for index in range(TILE // head_dim):
            total = jnp.sum(jnp.where(head == index, tile, 0.0), axis=1, keepdims=True)
            value = finish(total * (1.0 / head_dim))
            result = value if result is None else jnp.where(head == index, value, result)
        tiles.append(jnp.broadcast_to(result, tile.shape))
    return jnp.concatenate(tiles, axis=1)


def unit_rows(array, head_dim):
    scale = over_heads(array * array, head_dim, lambda mean: lax.rsqrt(mean + EPSILON))
    return array * scale, scale


def norm_back(grad_normed, unit_vals, scale, gain_row, head_dim):
    grad_unit = grad_normed * gain_row
    mean_inner = over_heads(grad_unit * unit_vals, head_dim, lambda mean: mean)
    return scale * (grad_unit - unit_vals * mean_inner)


def gain_lanes(gain_ref, width):
    row = gain_ref[...]
    return jnp.concatenate([row] * (width // row.shape[1]), axis=1)


def merge_kernel(head_dim, bounds, other, key_ref, value_ref, cells_ref, gain_ref, *refs):
    count = len(bounds)
    out_refs = refs[:count]
    key_buf, value_buf, cells_buf, gain_buf, copied = refs[count:]
    tok, half = key_buf.shape
    cells = cells_ref.shape[1]
    side = core_side()
    small = [
        pltpu.make_async_copy(cells_ref, cells_buf, copied.at[0]),
        pltpu.make_async_copy(gain_ref, gain_buf, copied.at[1]),
    ]
    for move in small:
        move.start()
    spans = [
        (chunk, start, stop, start + at, start + to)
        for chunk, (start, stop) in enumerate(bounds)
        for at, to in pieces(stop - start)
    ]
    moves = []
    for index, (_, _, _, at, to) in enumerate(spans):
        source = lanes_at((1 - side if other else side) * (half // TILE) + at // TILE, to - at)
        here = slice(at, to)
        for which, (far, near) in enumerate(((key_ref, key_buf), (value_ref, value_buf))):
            move = pltpu.make_async_copy(
                far.at[:, source], near.at[:, here], copied.at[2 + 2 * index + which]
            )
            move.start()
            moves.append(move)
    for move in small + moves:
        move.wait()
    listed = lax.rem(cells_buf[...], tok)
    ids = lax.broadcasted_iota(jnp.int32, (tok, cells), 0)
    member = sum((listed[j : j + 1] == ids).astype(F32) for j in range(cells_ref.shape[0]))
    member = member.T.astype(BF16)
    twice = jnp.concatenate([member, member], axis=1)
    for chunk, start, stop, at, to in spans:
        here = slice(at, to)
        out_ref = out_refs[chunk]
        unit_vals, _ = unit_rows(key_buf[:, here].astype(F32), head_dim)
        keys = dot(twice, jnp.concatenate(halves(unit_vals), axis=0))
        keys *= gain_lanes(gain_buf, to - at) * 0.25
        out_ref[:, at - start : to - start] = keys.astype(BF16)
        values = dot(member, value_buf[:, here]) * 0.25
        out_ref[:, stop - 2 * start + at : stop - 2 * start + to] = values.astype(BF16)


def pack_kernel(query_ref, upstream_ref, send_ref, copied):
    half = query_ref.shape[1] // CORES
    source = lanes_at((1 - core_side()) * (half // TILE), half)
    moves = [
        pltpu.make_async_copy(query_ref.at[:, source], send_ref.at[:, :half], copied.at[0]),
        pltpu.make_async_copy(upstream_ref.at[:, source], send_ref.at[:, half:], copied.at[1]),
    ]
    for move in moves:
        move.start()
    for move in moves:
        move.wait()


def query_kernel(
    head_dim, query_ref, upstream_ref, arrived_ref, gain_ref, unit_ref, scale_ref, *refs
):
    out_ref, grad_ref, copied = refs
    tok, lanes = query_ref.shape
    half = lanes // CORES
    side = core_side()
    source = lanes_at(side * (half // TILE), half)
    move = pltpu.make_async_copy(upstream_ref.at[:, source], grad_ref.at[:tok], copied.at[0])
    move.start()
    grad_ref[tok:] = arrived_ref[:, half:]
    for at, to in pieces(half):
        for row, queries in (
            (0, query_ref[:, lanes_at(side * (half // TILE) + at // TILE, to - at)]),
            (tok, arrived_ref[:, at:to]),
        ):
            here = slice(row, row + tok)
            unit_vals, scale = unit_rows(queries.astype(F32), head_dim)
            unit_ref[here, at:to] = unit_vals
            scale_ref[here, at:to] = scale
            out_ref[here, at:to] = (unit_vals * gain_lanes(gain_ref, to - at)).astype(BF16)
    move.wait()


def key_kernel(head_dim, key_ref, unmerge_ref, gain_ref, unit_ref, scale_ref, table_ref, row_ref):
    tok = key_ref.shape[0]
    cells = table_ref.shape[1] // 2
    owner = lax.rem(unmerge_ref[...], cells)
    table = (lax.broadcasted_iota(jnp.int32, (cells, tok), 0) == owner).astype(F32) * 0.25
    table = table.T.astype(BF16)
    table_ref[...] = jnp.concatenate([table, table], axis=1)
    row_ref[...] = gain_lanes(gain_ref, row_ref.shape[1])
    for at, to in pieces(key_ref.shape[1]):
        unit_vals, scale = unit_rows(key_ref[:, at:to].astype(F32), head_dim)
        unit_ref[:, at:to] = unit_vals
        scale_ref[:, at:to] = scale


def attend_kernel(head_dim, start, blocks, group, *refs):
    query_ref, upstream_ref, unit_ref, scale_ref, gain_ref = refs[:5]
    block_refs = refs[5 : 5 + blocks]
    own_ref, send_ref, gain_out_ref = refs[5 + blocks : 8 + blocks]
    part_refs = refs[8 + blocks :]
    rows = query_ref.shape[0]
    block_rows, width = block_refs[0].shape
    width = width // 2
    per = TILE // head_dim
    cells = group * block_rows
    scale = head_dim**-0.5
    exponent = scale * math.log2(math.e)
    lane_head = lax.broadcasted_iota(jnp.int32, (1, TILE), 1) // head_dim
    cell_heads = lax.broadcasted_iota(jnp.int32, (cells, TILE), 1) // head_dim
    masks = [(cell_heads == head).astype(F32).astype(BF16) for head in range(per)]

    heads = range(per)

    def spread(array):
        return jnp.concatenate([array * mask for mask in masks], axis=0)

    def by_lane(parts):
        result = parts[0]
        for head in range(1, per):
            result = jnp.where(lane_head == head, parts[head], result)
        return result

    def per_head(left, rights, contract):
        return jnp.concatenate(
            [
                dot(left[h * head_dim : (h + 1) * head_dim], rights[h], ((1,), (contract,)))
                for h in heads
            ],
            axis=0,
        ).T

    def forward(tile):
        lane = lanes_at(tile)
        value_lane = lanes_at(width // TILE + tile)
        source = lanes_at(start // TILE + tile)
        queries = query_ref[:, source]
        upstream = upstream_ref[:, source]
        weighted = jnp.zeros((rows, TILE), F32)
        totals = [jnp.zeros((rows, 1), F32) for _ in heads]
        held = []
        for first in range(0, blocks, group):
            members = block_refs[first : first + group]
            keys = jnp.concatenate([ref[:, lane] for ref in members], axis=0)
            values = jnp.concatenate([ref[:, value_lane] for ref in members], axis=0)
            scores = dot(queries, spread(keys), ((1,), (1,)))
            exp_scores = jnp.exp2(scores * exponent)
            exp_parts = [exp_scores[:, h * cells : (h + 1) * cells] for h in heads]
            weighted += dot(exp_scores.astype(BF16), spread(values))
            totals = [
                total + jnp.sum(part, axis=1, keepdims=True)
                for total, part in zip(totals, exp_parts)
            ]
            held.append((keys, dot(upstream, spread(values), ((1,), (1,))), exp_parts))
        inverses = [1.0 / total for total in totals]
        attended = (weighted * by_lane(inverses)).astype(BF16)
        own_ref[:, lane] = attended[: rows // CORES]
        send_ref[:, lane] = attended[rows // CORES :]
        products = upstream.astype(F32) * attended.astype(F32)
        inners = [
            jnp.sum(jnp.where(lane_head == h, products, 0.0), axis=1, keepdims=True) for h in heads
        ]
        return queries, upstream, held, inverses, inners

    def backward(tile, kept, sums):
        query_sum, key_sum = sums
        queries, upstream, held, inverses, inners = kept
        lane = lanes_at(tile)
        value_lane = lanes_at(width // TILE + tile)
        queries_turned, upstream_turned = queries.T, upstream.T
        grad_queries = jnp.zeros((rows, TILE), F32)
        for index, (keys, grad_weights, exp_parts) in enumerate(held):
            attention = [part * inverse for part, inverse in zip(exp_parts, inverses)]
            grad_scores = [
                (attention[h] * (grad_weights[:, h * cells : (h + 1) * cells] - inners[h])).astype(
                    BF16
                )
                for h in heads
            ]
            grad_queries += dot(jnp.concatenate(grad_scores, axis=1), spread(keys))
            grad_keys = per_head(queries_turned, grad_scores, 0) * scale
            grad_values = per_head(upstream_turned, [part.astype(BF16) for part in attention], 0)
            key_sum += jnp.sum(grad_keys * keys.astype(F32), axis=0, keepdims=True)
            for member in range(group):
                ref = part_refs[index * group + member]
                here = slice(member * block_rows, (member + 1) * block_rows)
                ref[:, lane] = grad_keys[here].astype(ref.dtype)
                ref[:, value_lane] = grad_values[here].astype(ref.dtype)
        grad_queries *= scale
        grads = norm_back(
            grad_queries,
            unit_ref[:, lanes_at(start // TILE + tile)],
            scale_ref[:, lanes_at(start // TILE + tile)],
            gain_lanes(gain_ref, TILE),
            head_dim,
        ).astype(BF16)
        own_ref[:, value_lane] = grads[: rows // CORES]
        send_ref[:, value_lane] = grads[rows // CORES :]
        query_sum += jnp.sum(grad_queries * queries.astype(F32), axis=0, keepdims=True)
        return query_sum, key_sum

    sums = (jnp.zeros((1, TILE), F32), jnp.zeros((1, TILE), F32))
    if blocks == group:
        kept = forward(0)
        for tile in range(width // TILE):
            ahead = forward(tile + 1) if tile + 1 < width // TILE else None
            sums = backward(tile, kept, sums)
            kept = ahead
    else:
        sums = lax.fori_loop(
            0, width // TILE, lambda tile, sums: backward(tile, forward(tile), sums), sums
        )

    def per_channel(row):
        return sum(row[:, at : at + head_dim] for at in range(0, TILE, head_dim))

    gain_out_ref[...] = jnp.concatenate([per_channel(row) for row in sums], axis=1)


def place_kernel(bounds, *refs):
    count = len(bounds)
    own_refs, outs, copied = refs[:count], refs[count : count + 2], refs[count + 2]
    half = bounds[-1][1]
    moves = []
    for (start, stop), own_ref in zip(bounds, own_refs):
        width = stop - start
        place = lanes_at(core_side() * (half // TILE) + start // TILE, width)
        for index, out in enumerate(outs):
            source = own_ref.at[:, index * width : (index + 1) * width]
            moves.append(pltpu.make_async_copy(source, out.at[:, place], copied.at[len(moves)]))
            moves[-1].start()
    for move in moves:
        move.wait()


def key_back_kernel(head_dim, bounds, own_terms, other_terms, *refs):
    query_refs, refs = refs[2 : 2 + len(bounds)], refs[2 + len(bounds) :]
    unit_ref, scale_ref, table_ref, gain_ref = refs[:4]
    refs = refs[4:]
    sources = []
    for _ in bounds:
        sources.append((refs[:own_terms], refs[own_terms : own_terms + other_terms]))
        refs = refs[own_terms + other_terms :]
    grad_key_out, grad_value_out, *query_outs, grad_key_buf, grad_value_buf, copied = refs
    tok, half = grad_key_buf.shape[1:]
    cells = sources[0][1][0].shape[0]
    side = core_side()
    table = table_ref[...]

    def spread(chunk, other, at, to):
        total = added([ref[:cells, at:to] for ref in sources[chunk][other]])
        return dot(table, jnp.concatenate(halves(total), axis=0))

    spans = [
        (other, chunk, start, stop, start + at, start + to)
        for other in range(CORES)
        for chunk, (start, stop) in enumerate(bounds)
        for at, to in pieces(stop - start)
    ]
    moves = []

    def send(buf, out, other, start=0, width=half):
        first = (1 - side if other else side) * (half // TILE)
        place = lanes_at(first + start // TILE, width)
        move = pltpu.make_async_copy(buf, out.at[:, place], copied.at[len(moves)])
        move.start()
        moves.append(move)

    for (start, stop), ref in zip(bounds, query_refs):
        width = stop - start
        for index, out in enumerate(query_outs):
            send(ref.at[:, index * width : (index + 1) * width], out, 1, start, width)
    for other, chunk, start, stop, at, to in spans:
        grad_value_buf[other, :, at:to] = spread(
            chunk, other, stop - 2 * start + at, stop - 2 * start + to
        ).astype(BF16)
    for other in range(CORES):
        send(grad_value_buf.at[other], grad_value_out, other)
    for other, chunk, start, stop, at, to in spans:
        first = (1 - side if other else side) * (half // TILE)
        lane = lanes_at(first + at // TILE, to - at)
        grad_key_buf[other, :, at:to] = norm_back(
            spread(chunk, other, at - start, to - start),
            unit_ref[:, lane],
            scale_ref[:, lane],
            gain_ref[:, : to - at],
            head_dim,
        ).astype(BF16)
        if to == half:
            send(grad_key_buf.at[other], grad_key_out, other)
    for move in moves:
        move.wait()


def exchange(array, axis, apart):
    return lax.ppermute(array, axis, [(i, i ^ apart) for i in range(lax.axis_size(axis))])


def chip_gather(block, chips):
    if chips == 1:
        return [block]
    mirrored = exchange(block, "seq", CORES * (chips - 1))
    return chip_gather(block, chips // 2) + chip_gather(mirrored, chips // 2)[::-1]


def chip_reduce(parts):
    chips = len(parts)
    if chips == 1:
        return [parts[0]]
    sent = added(chip_reduce(parts[: chips // 2 - 1 : -1])).astype(BF16)
    return chip_reduce(parts[: chips // 2]) + [exchange(sent, "seq", CORES * (chips - 1))]


def added(terms):
    total = terms[0].astype(F32)
    for term in terms[1:]:
        total += term.astype(F32)
    return total


class Rest:
    def __init__(self, gains, chips):
        self.gains = gains
        images = lax.axis_size("img")
        image_steps = [("img", 1 << bit) for bit in range(images.bit_length() - 1)]
        chip_steps = [("seq", CORES << bit) for bit in range(chips.bit_length() - 1)]
        self.table = {
            "c": [("seq", 1)],
            "I": [("img", *range(1, images))],
            "y": image_steps[:1],
            "x": image_steps[1:],
            "z": chip_steps[:1],
            "w": chip_steps[1:],
            "D": [("seq", *(CORES * apart for apart in range(1, chips)))],
        }

    def advance(self, names):
        for name in names:
            for axis, *aparts in self.table[name]:
                arrived = [exchange(self.gains, axis, apart) for apart in aparts]
                self.gains = sum(arrived, self.gains)


OPT = dict(tl=2, kk=1, km=2.0, tp=0, tc=1, split=0, steps="D|yxc|", near=1, hb=0, sb=2, pc=0.1)


def chunk_bounds(half):
    return ((0, half),)


def local(query_proj, key_proj, value_proj, merge_cells, unmerge, grad_out, query_gain, key_gain):
    queries, key_rows, value_rows = query_proj[0], key_proj[0], value_proj[0]
    upstream = grad_out[0]
    tok, lanes = queries.shape
    half = lanes // CORES
    head_dim = query_gain.shape[0]
    cells = merge_cells.shape[1]
    chips = lax.axis_size("seq") // CORES
    bounds = chunk_bounds(half)
    widths = [stop - start for start, stop in bounds]
    query_row, key_row = query_gain[None], key_gain[None]

    def merged_half(other):
        return call(
            functools.partial(merge_kernel, head_dim, bounds, other),
            [((cells, 2 * width), BF16) for width in widths],
            [key_rows, value_rows, merge_cells[0].T, key_row],
            scratch=[((tok, half), BF16)] * 2
            + [(merge_cells.shape[:0:-1], jnp.int32), ((1, head_dim), F32)],
            far_in=4,
            copies=2 + 2 * sum(len(pieces(width)) for width in widths),
            vmem=ALL_VMEM_BYTES if other else OWN_VMEM_BYTES,
            micros=0.5,
        )

    sent_half = merged_half(True)
    merged = merged_half(False)
    crossed = [exchange(sent, "seq", 1) for sent in sent_half]
    crossed, late_queries, late_upstream, late_keys = lax.optimization_barrier(
        (crossed, queries, upstream, key_rows)
    )
    gathered = [
        chip_gather(jnp.concatenate([own, other], axis=0), chips)
        for own, other in zip(merged, crossed)
    ]

    (packed,) = call(
        pack_kernel, [((tok, lanes), BF16)], [late_queries, late_upstream], far_in=2, copies=2
    )
    query_unit, query_scale, normed, both_upstream = call(
        functools.partial(query_kernel, head_dim),
        [((CORES * tok, half), F32)] * 2 + [((CORES * tok, half), BF16)] * 2,
        [queries, upstream, exchange(packed, "seq", 1), query_row],
        copies=1,
    )
    key_unit, key_scale, table, gain_row = call(
        functools.partial(key_kernel, head_dim),
        [((tok, lanes), F32)] * 2 + [((tok, 2 * cells), BF16), ((1, 2 * TILE), F32)],
        [late_keys, unmerge, key_row],
    )

    if OPT["kk"]:
        normed, key_unit, key_scale, table, gain_row = lax.optimization_barrier(
            (normed, key_unit, key_scale, table, gain_row)
        )
    group = min(chips, 4)
    results = [
        call(
            functools.partial(attend_kernel, head_dim, start, chips, group),
            [
                ((tok, 2 * width), BF16),
                ((tok, 2 * width), BF16),
                ((1, 2 * head_dim), F32),
                ((CORES * cells, 2 * width), F32),
            ]
            + [((CORES * cells, 2 * width), BF16)] * (chips - 1),
            [normed, both_upstream, query_unit, query_scale, query_row] + blocks,
            micros=3.5 * width / half,
        )
        for (start, stop), width, blocks in zip(bounds, widths, gathered)
    ]
    rest = Rest(sum(result[2] for result in results), chips)

    first_steps, next_steps, last_steps = OPT["steps"].split("|")

    parts = [result[3:] for result in results]
    far = [chip_reduce(part[: chips // 2 - 1 : -1]) if chips > 1 else [] for part in parts]
    rest.advance(first_steps[:1])
    near_parts = [part[: max(chips // 2, 1)] for part in parts]
    if OPT["tp"] == 1:
        _, near_parts = lax.optimization_barrier((rest.gains, near_parts))
    rest.advance(first_steps[1:])
    if OPT["tp"] == 2:
        _, near_parts = lax.optimization_barrier((rest.gains, near_parts))
    if OPT["hb"]:
        far, rest.gains = lax.optimization_barrier((far, rest.gains))
    mirror = CORES * (chips - 1)
    sums = [added(terms).astype(BF16) for terms in far if terms]
    if OPT["sb"] == 1:
        sums, rest.gains = lax.optimization_barrier((sums, rest.gains))
    if OPT["sb"] == 2:
        _, rest.gains = lax.optimization_barrier((sums, rest.gains))
    if OPT["split"]:
        straight = [[exchange(sent[:cells], "seq", mirror)] for sent in sums]
        across = [[exchange(sent[cells:], "seq", mirror + 1)] for sent in sums]
    else:
        straight = [[exchange(sent, "seq", mirror)] for sent in sums]
        across = [[] for _ in bounds]
    if chips == 1:
        straight = across = [[] for _ in bounds]
    near = [chip_reduce(part) for part in near_parts]
    if OPT["tc"]:
        near_crossed = [exchange(added([t[cells:] for t in terms]), "seq", 1) for terms in near]
    if OPT["split"]:
        crossed = [exchange(added([term[cells:] for term in terms]), "seq", 1) for terms in near]
    else:
        crossed = None
    if OPT["near"] == 1:
        rest.advance(next_steps[:1])
        near, rest.gains = lax.optimization_barrier((near, rest.gains))
        rest.advance(next_steps[1:])
    elif OPT["near"] == 2:
        near, rest.gains = lax.optimization_barrier((near, rest.gains))
        rest.advance(next_steps)
    else:
        rest.advance(next_steps)
    arrived_part = [exchange(result[1], "seq", 1) for result in results]
    attended_half, grad_half = call(
        functools.partial(place_kernel, bounds),
        [((tok, lanes), BF16)] * 2,
        [result[0] for result in results],
        far_out=2,
        copies=2 * len(bounds),
        micros=OPT["pc"],
    )
    if OPT["tl"] == 1:
        straight, rest.gains = lax.optimization_barrier((straight, rest.gains))
    elif OPT["tl"] == 2:
        pass
    elif OPT["tc"]:
        straight, near_crossed, rest.gains, arrived_part = lax.optimization_barrier(
            (straight, near_crossed, rest.gains, arrived_part)
        )
    else:
        straight, rest.gains, arrived_part = lax.optimization_barrier(
            (straight, rest.gains, arrived_part)
        )
    own_terms = [first + last for first, last in zip(near, straight)]
    if OPT["tc"] and chips > 1:
        crossed = near_crossed
        across = [[exchange(term[cells:], "seq", 1) for term in terms] for terms in straight]
    elif not OPT["split"]:
        crossed = [exchange(added([t[cells:] for t in terms]), "seq", 1) for terms in own_terms]
    if OPT["tl"] == 2:
        across, rest.gains = lax.optimization_barrier((across, rest.gains))
    rest.advance(last_steps)
    gain_total = rest.gains[0]

    sources = []
    for chunk in range(len(bounds)):
        sources += own_terms[chunk] + [crossed[chunk]] + across[chunk]
    grad_key, grad_value, attended_all, grad_query = call(
        functools.partial(key_back_kernel, head_dim, bounds, len(own_terms[0]), 1 + len(across[0])),
        [((tok, lanes), BF16)] * 4,
        [attended_half, grad_half]
        + arrived_part
        + [key_unit, key_scale, table, gain_row]
        + sources,
        scratch=[((CORES, tok, half), BF16)] * 2,
        far_in=2,
        far_out=4,
        copies=2 * CORES + 2 * len(bounds),
        aliases={0: 2, 1: 3},
        micros=OPT["km"],
    )
    return (
        attended_all[None],
        grad_query[None],
        grad_key[None],
        grad_value[None],
        gain_total[:head_dim] / query_gain,
        gain_total[head_dim:] / key_gain,
    )


def solution(mesh):
    rows = P("img", "seq", None)
    return jax.shard_map(
        local,
        mesh=mesh,
        in_specs=(rows, rows, rows, rows, P("img", "seq"), rows, P(), P()),
        out_specs=(rows, rows, rows, rows, P(), P()),
        check_vma=False,
    )
```
